512 devices in a mesh: seq: 128 (over z, y, core), head: 4 (over x).
Axes of the slice: x: 4, y: 8, z: 8, core: 2. Of those that a mesh axis runs over, the one named last changes fastest.
Arguments:
- alignment: bfloat16 [128, 768, 256], P('seq', 'head'), may hold values from -6 to 6
- row_query_key: bfloat16 [2, 768, 768], P(None, 'head'), may hold values from -1 to 1, as said below
- row_value: bfloat16 [768, 768], P('head'), may hold values from -0.21875 to 0.21875
- row_output: bfloat16 [768, 768], P('head'), may hold values from -1.25 to 1.25
- col_query_key: bfloat16 [2, 768, 768], P(None, 'head'), may hold values from -10 to 10, as said below
- col_value: bfloat16 [768, 768], P('head'), may hold values from -0.21875 to 0.21875
- col_output: bfloat16 [768, 768], P('head'), may hold values from -1.25 to 1.25
- sequence_mask: int32 [128], replicated, may hold values from 0 to 1, as said below
- residue_mask: int32 [256], replicated, may hold values from 0 to 1, as said below
Outputs:
- layer_output: bfloat16 [128, 768, 256], P('seq', 'head')
The draws below stay inside these ranges and needn't reach their ends.
Inputs may be any that keep to these rules, and one draw needn't show every extreme that they name: `sequence_mask`: 64 or more ones and at least one zero, at any positions. `residue_mask`: the ones form a prefix of 128 or more entries; the rest are zeros, at least one. `row_query_key`: query projection first, key projection second. `col_query_key`: query projection first, key projection second.
All inputs are finite; a program needn't handle non-finite values.
Results may differ from the reference program's by a relative error of at most 0.025.
Values may be sent and summed in bfloat16 or wider, within the bound.
A program may use at most 64 MiB of HBM per device.

```python
import math
import jax
import jax.numpy as jnp
from jax import lax

D = 768
HEADS = 12
L = 256
SEQS = 128


def normal_pair(key):
    return (jax.random.normal(key, (2, D, D), jnp.float32) * D ** (-0.5)).astype(jnp.bfloat16)


def draw_row_query_key(key, part):
    key = jax.random.fold_in(key, 1)
    return normal_pair(key)


def draw_col_query_key(key, part):
    key = jax.random.fold_in(key, 2)
    return normal_pair(key)


def draw_sequence_mask(key, part):
    key = jax.random.fold_in(key, 3)
    count_key, order_key = jax.random.split(key)
    live_count = jax.random.randint(count_key, (), SEQS // 2, SEQS)
    order = jax.random.permutation(order_key, SEQS)
    return (order < live_count).astype(jnp.int32)


def draw_residue_mask(key, part):
    key = jax.random.fold_in(key, 4)
    live_count = jax.random.randint(key, (), L // 2, L)
    return (jnp.arange(L, dtype=jnp.int32) < live_count).astype(jnp.int32)


def level_of(key, dims, shards, least, largest):
    factor_of = 1.0
    for dim, parts in shards:
        draws = jax.random.uniform(jax.random.fold_in(jax.random.fold_in(key, 6), dim), (parts,), jnp.float32, least / len(shards), largest / len(shards))
        factor_of = factor_of * jnp.repeat(jnp.exp(draws), dims[dim] // parts).reshape((-1,) + (1,) * (len(dims) - 1 - dim))
    return factor_of


def scatter_about(stream_key, dims, deviation, bound, pieces=(), kind=jnp.bfloat16):
    drawn = deviation * jax.random.normal(stream_key, dims, jnp.float32)
    if pieces:
        drawn = drawn * level_of(stream_key, dims, pieces, -0.22, 0.18)
    return jnp.clip(drawn, -bound, bound).astype(kind)


def setup_inputs(seed: int = 0) -> dict:
    key_of = jax.random.split(jax.random.key(seed), 10)
    return {
        "alignment": scatter_about(key_of[0], (SEQS, D, L), 1.0, 6.0, ((0, 128), (1, 4))),
        "row_query_key": draw_row_query_key(jax.random.fold_in(key_of[9], 71), 0),
        "row_value": scatter_about(key_of[2], (D, D), D ** -0.5, 0.21875, ((0, 4),)),
        "row_output": scatter_about(key_of[3], (D, D), (D // 32) ** -0.5, 1.25, ((0, 4),)),
        "col_query_key": draw_col_query_key(jax.random.fold_in(key_of[9], 71), 0),
        "col_value": scatter_about(key_of[5], (D, D), D ** -0.5, 0.21875, ((0, 4),)),
        "col_output": scatter_about(key_of[6], (D, D), (D // 32) ** -0.5, 1.25, ((0, 4),)),
        "sequence_mask": draw_sequence_mask(jax.random.fold_in(key_of[9], 71), 0),
        "residue_mask": draw_residue_mask(jax.random.fold_in(key_of[9], 71), 0),
    }


EPSILON = 1e-05
MASKED = -1e+30

def normalize(values):
    floats = values.astype(jnp.float32)
    centred = floats - lax.optimization_barrier(jnp.mean(floats, axis=-1, keepdims=True))
    variance = lax.optimization_barrier(jnp.mean(centred * centred, axis=-1, keepdims=True))
    return (centred * lax.rsqrt(variance + EPSILON)).astype(jnp.bfloat16)

def masked_softmax(logits, live):
    return jax.nn.softmax(jnp.where(live, logits, MASKED), axis=-1).astype(jnp.bfloat16)

def times_weight(rows, weights):
    return lax.dot_general(rows, weights, (((1,), (1,)), ((), ())), preferred_element_type=jnp.float32)

def project(normed, weights):
    head_size = D // HEADS
    product = times_weight(normed, weights)
    return product.reshape(SEQS, L, HEADS, head_size)

def reference(alignment, row_query_key, row_value, row_output, col_query_key, col_value, col_output, sequence_mask, residue_mask):
    head_size = D // HEADS
    flat_rows = SEQS * L
    row_stream = alignment.transpose(0, 2, 1)
    seq_live = sequence_mask.astype(jnp.float32).reshape(SEQS, 1, 1, 1)
    key_live = (residue_mask > 0)[None, :]
    normed = normalize(row_stream).reshape(flat_rows, D)
    queries = (project(normed, row_query_key[0]) * seq_live).astype(jnp.bfloat16)
    key_rows = project(normed, row_query_key[1]).astype(jnp.bfloat16)
    value_rows = project(normed, row_value).astype(jnp.bfloat16)
    logit_scale = head_size ** (-0.5) / math.sqrt(SEQS)

    def row_head(operands):
        head_queries, head_keys, head_values = operands
        logits = jnp.einsum('sid,sjd->ij', head_queries.astype(jnp.float32), head_keys.astype(jnp.float32)) * logit_scale
        row_probs = masked_softmax(logits, key_live)
        context = jnp.einsum('ij,sjd->sid', row_probs.astype(jnp.float32), head_values.astype(jnp.float32))
        return context.astype(jnp.bfloat16)
    stacked = lax.map(row_head, (queries.transpose(2, 0, 1, 3), key_rows.transpose(2, 0, 1, 3), value_rows.transpose(2, 0, 1, 3)))
    row_context = stacked.transpose(1, 2, 0, 3).reshape(flat_rows, D)
    row_mixed = times_weight(row_context, row_output).reshape(SEQS, L, D)
    stream = (row_stream.astype(jnp.float32) + row_mixed).astype(jnp.bfloat16)
    col_normed = normalize(stream).reshape(flat_rows, D)
    col_queries = project(col_normed, col_query_key[0]).astype(jnp.bfloat16)
    col_keys = project(col_normed, col_query_key[1]).astype(jnp.bfloat16)
    col_values = project(col_normed, col_value).astype(jnp.bfloat16)
    seq_keys = (sequence_mask > 0)[None, None, :]

    def col_head(operands):
        head_queries, head_keys, head_values = operands
        logits = jnp.einsum('sid,tid->ist', head_queries.astype(jnp.float32), head_keys.astype(jnp.float32)) * head_size ** (-0.5)
        col_probs = masked_softmax(logits, seq_keys)
        context = jnp.einsum('ist,tid->sid', col_probs.astype(jnp.float32), head_values.astype(jnp.float32))
        return context.astype(jnp.bfloat16)
    col_stacked = lax.map(col_head, (col_queries.transpose(2, 0, 1, 3), col_keys.transpose(2, 0, 1, 3), col_values.transpose(2, 0, 1, 3)))
    col_context = col_stacked.transpose(1, 2, 0, 3).reshape(flat_rows, D)
    col_mixed = times_weight(col_context, col_output).reshape(SEQS, L, D)
    result = (stream.astype(jnp.float32) + col_mixed).astype(jnp.bfloat16)
    return result.transpose(0, 2, 1)
```

```python
import math

import jax
import jax.numpy as jnp
from jax import lax
from jax.experimental import pallas as pl
from jax.experimental.pallas import tpu as pltpu
from jax.sharding import PartitionSpec as P

D = 768
HEADS = 12
L = 256
SEQS = 128
HEAD = D // HEADS
PART = D // 4
EPSILON = 1e-05
MASKED = -1e30
ROW_SCALE = HEAD**-0.5 / math.sqrt(SEQS)
COL_SCALE = HEAD**-0.5
MESH = pl.DeviceIdType.MESH
BF16 = jnp.bfloat16
F32 = jnp.float32


def dot_nt(a, b):
    return lax.dot_general(a, b, (((1,), (1,)), ((), ())), preferred_element_type=F32)


def dot_nn(a, b):
    return lax.dot_general(a, b, (((1,), (0,)), ((), ())), preferred_element_type=F32)


def dot_tn(a, b):
    return lax.dot_general(a, b, (((0,), (0,)), ((), ())), preferred_element_type=F32)


def normalize(values, axis):
    centred = values - jnp.mean(values, axis=axis, keepdims=True)
    variance = jnp.mean(centred * centred, axis=axis, keepdims=True)
    return (centred * lax.rsqrt(variance + EPSILON)).astype(BF16)


def softmax(logits, live):
    logits = jnp.where(live, logits, MASKED)
    weights = jnp.exp(logits - jnp.max(logits, axis=-1, keepdims=True))
    return (weights / jnp.sum(weights, axis=-1, keepdims=True)).astype(BF16)


def rounded(values):
    return values.astype(BF16).astype(F32)


def layer(
    al, rqk, rv, ro, cqk, cv, co, smask, rmask, out,
    ag, wrow, wfull, qh, kk, vv, qrx, krx, vrx, pacc, pb, ra, sb, rb, pf,
    ctxb, cx, srow, rx, kf, vf, xb, xr, mrow, mrx,
    lsem, xs_s, xs_r, wg_s, wg_r, wf_s, wf_r, co_s, co_r, ra_s, ra_r, rb_s, rb_r,
    pa_s, pa_r, cx_s, cx_r, aa_s, aa_r, kv_s, kv_r, ox_s, ox_r, bb_s, bb_r,
):
    s = lax.axis_index("seq")
    x = lax.axis_index("head")
    z, y, c = s // 16, (s // 2) % 8, s % 2
    zy = z * 8 + y
    first = c == 0
    ia = jnp.where(first, y, z)
    ib = jnp.where(first, z, y)

    def dev(z_, y_, c_, x_):
        return (z_ * 16 + y_ * 2 + c_, x_)

    def dev_a(g):
        return dev(jnp.where(first, z, g), jnp.where(first, g, y), c, x)

    def dev_b(g):
        return dev(jnp.where(first, g, z), jnp.where(first, y, g), c, x)

    def remote(src, dst, ss, rs, target):
        return pltpu.make_async_remote_copy(
            src_ref=src, dst_ref=dst, send_sem=ss, recv_sem=rs, device_id=target, device_id_type=MESH
        )

    sibling = dev(z, y, 1 - c, x)

    mine = pl.ds(pl.multiple_of(PART * x, 64), PART)
    weights = (ro, cqk.at[1], cv, cqk.at[0], co)
    loads = [pltpu.make_async_copy(al.at[0], ag.at[x], lsem.at[0])]
    for i, ref in enumerate((rqk.at[0], rqk.at[1], rv)):
        loads.append(pltpu.make_async_copy(ref, wrow.at[i], lsem.at[1 + i]))
    for i, ref in enumerate(weights):
        loads.append(pltpu.make_async_copy(ref, wfull.at[i, mine, :], lsem.at[4 + i]))
    for copy in loads:
        copy.start()

    barrier = pltpu.get_barrier_semaphore()
    greeted = [dev_a((ia + k) % 8) for k in range(1, 8)] + [dev_b((ib + k) % 8) for k in range(1, 8)]
    greeted += [dev(z, y, (c + j) % 2, (x + k) % 4) for k in range(4) for j in range(2) if j or k]
    for target in greeted:
        pl.semaphore_signal(barrier, inc=1, device_id=target, device_id_type=MESH)
    loads[0].wait()
    pl.semaphore_wait(barrier, len(greeted))

    gathers = {}
    for k in (2, 1, 3):
        gathers[k] = remote(ag.at[x], ag.at[x], xs_s.at[k - 1], xs_r.at[k - 1], dev(z, y, c, (x + k) % 4))
        gathers[k].start()
    for copy in loads[1:]:
        copy.wait()
    for k in (1, 3, 2):
        gathers[k].wait_recv()

    floats = ag[...].reshape(D, L).astype(F32)
    normed = normalize(floats, 0)
    live = jnp.sum(
        jnp.where(lax.broadcasted_iota(jnp.int32, (1, SEQS), 1) == s, smask[...], 0), axis=-1, keepdims=True
    ).astype(F32)
    keys = dot_nn(wrow[1], normed).astype(BF16)
    kk[...] = keys
    queries = (dot_nn(wrow[0], normed) * live).astype(BF16)
    qh[0] = queries[:, :128]
    qh[1] = queries[:, 128:]
    swaps = [
        remote(kk, krx, co_s.at[0], co_r.at[0], sibling),
        remote(qh.at[1 - c], qrx, co_s.at[1], co_r.at[1], sibling),
        remote(vv, vrx, co_s.at[2], co_r.at[2], sibling),
    ]
    swaps[0].start()
    swaps[1].start()
    vv[...] = dot_nn(wrow[2], normed).astype(BF16)
    swaps[2].start()

    own_q = qh[c]
    for h in range(3):
        r = slice(HEAD * h, HEAD * h + HEAD)
        pacc[128 * h : 128 * h + 128, :] = dot_tn(own_q[r], keys[r])
    swaps[0].wait_recv()
    swaps[1].wait_recv()
    for h in range(3):
        r = slice(HEAD * h, HEAD * h + HEAD)
        total = pacc[128 * h : 128 * h + 128, :] + dot_tn(qrx[r, :], krx[r, :])
        pacc[128 * h : 128 * h + 128, :] = total
        pb[128 * h : 128 * h + 128, :] = total.astype(BF16)

    def chunk(g):
        return pl.ds(pl.multiple_of(48 * g, 16), 48)

    scatters = {}
    for k in (4, 3, 5, 2, 6, 1, 7):
        g = (ia + k) % 8
        scatters[k] = remote(pb.at[chunk(g), :], ra.at[k - 1], ra_s.at[k - 1], ra_r.at[k - 1], dev_a(g))
        scatters[k].start()

    half = pl.ds(pl.multiple_of(PART * x + 96 * c, 32), 96)
    wgather = [[None] * 3 for _ in range(5)]
    for i in range(5):
        for k in (1, 3, 2):
            copy = remote(
                wfull.at[i, half, :], wfull.at[i, half, :], wg_s.at[i, k - 1], wg_r.at[i, k - 1],
                dev(z, y, c, (x + k) % 4),
            )
            copy.start()
            wgather[i][k - 1] = copy

    def forward(i):
        copies = []
        for k in (1, 2, 3):
            wgather[i][k - 1].wait_recv()
            rows = pl.ds(pl.multiple_of(PART * ((x + 4 - k) % 4) + 96 * c, 32), 96)
            copy = remote(
                wfull.at[i, rows, :], wfull.at[i, rows, :], wf_s.at[i, k - 1], wf_r.at[i, k - 1], sibling
            )
            copy.start()
            copies.append(copy)
        return copies

    for k in (1, 7, 2, 6, 3, 5, 4):
        scatters[k].wait_recv()
    summed = pacc[pl.ds(pl.multiple_of(48 * ia, 16), 48), :]
    for k in range(7):
        summed = summed + ra[k].astype(F32)
    sb[...] = summed.astype(BF16)
    spreads = {}
    for k in (4, 3, 5, 2, 6, 1, 7):
        spreads[k] = remote(sb, rb.at[k - 1], rb_s.at[k - 1], rb_r.at[k - 1], dev_b((ib + k) % 8))
        spreads[k].start()
    pick = (
        lax.broadcasted_iota(jnp.int32, (64, L), 1) == lax.broadcasted_iota(jnp.int32, (64, L), 0) + 64 * x
    ).astype(BF16)
    quarter = jnp.concatenate([dot_nt(pick, ag[i]) for i in range(4)], axis=1)
    for k in (1, 7, 2, 6, 3, 5, 4):
        spreads[k].wait_recv()
    for k in range(7):
        summed = summed + rb[k].astype(F32)
    own_chunk = chunk(ia)
    pf[own_chunk, :] = softmax(summed * ROW_SCALE, rmask[...] > 0)
    probs = {}
    for k in (4, 3, 5, 2, 6, 1, 7):
        probs[k] = remote(
            pf.at[own_chunk, :], pf.at[own_chunk, :], pa_s.at[k - 1], pa_r.at[k - 1], dev_a((ia + k) % 8)
        )
        probs[k].start()
    forwards = [forward(0)]
    swaps[2].wait_recv()
    for k in (1, 7, 2, 6, 3, 5, 4):
        probs[k].wait_recv()

    mixed = []
    for h in range(3):
        r = slice(HEAD * h, HEAD * h + HEAD)
        both = jnp.concatenate([vv[r, :], vrx[r, :]], axis=0)
        mixed.append(dot_nt(pf[128 * h : 128 * h + 128, :], both))
    ctxb[0] = jnp.concatenate([m[:, :HEAD] for m in mixed], axis=1).astype(BF16)
    ctxb[1] = jnp.concatenate([m[:, HEAD:] for m in mixed], axis=1).astype(BF16)
    contexts = []
    for j in range(2):
        for q in range(2):
            src = ctxb.at[j, 64 * q : 64 * q + 64, :]
            owner = 2 * c + q
            copy = remote(src, cx.at[x], cx_s.at[2 * j + q], cx_r.at[x], dev(z, y, (c + j) % 2, owner))
            if j:
                copy.start()
                contexts.append((None, copy))
            else:
                here = owner == x

                @pl.when(here)
                def _():
                    pltpu.make_async_copy(src, cx.at[x], cx_r.at[x]).start()

                @pl.when(jnp.logical_not(here))
                def _():
                    copy.start()

                contexts.append((here, copy))
    for copy in forwards[0]:
        copy.wait_recv()
    for i in range(4):
        pltpu.make_async_copy(ctxb.at[0, :64, :], cx.at[i], cx_r.at[i]).wait()
    context = jnp.concatenate([cx[i].astype(F32) for i in range(4)], axis=1).astype(BF16)
    stream = rounded(quarter + dot_nt(context, wfull[0]))
    srow[...] = stream.reshape(64, 1, D)

    def exchange(src, dst, ss, rs):
        def send(step, carry):
            k = (step + 36) % 64
            z_, y_ = (z + k // 8) % 8, (y + k) % 8

            @pl.when(k != 0)
            def _():
                remote(src.at[z_ * 8 + y_], dst.at[zy], ss, rs, dev(z_, y_, c, x)).start()

            return carry

        lax.fori_loop(0, 64, send, 0)
        pltpu.make_async_copy(src.at[zy], dst.at[zy], rs).start()

    def exchanged(src, dst, ss, rs):
        pltpu.make_async_copy(src, dst, rs).wait()
        pltpu.make_async_copy(src.at[:63], dst.at[:63], ss).wait()

    exchange(srow, rx, aa_s.at[0], aa_r.at[0])
    for i in range(1, 5):
        forwards.append(forward(i))
    order = (
        lax.broadcasted_iota(jnp.int32, (SEQS, SEQS), 0)
        == (lax.broadcasted_iota(jnp.int32, (SEQS, SEQS), 1) % 64) * 2
        + lax.broadcasted_iota(jnp.int32, (SEQS, SEQS), 1) // 64
    ).astype(BF16)
    live_bits = jnp.broadcast_to((smask[...] > 0).astype(BF16), (16, SEQS))
    seq_keys = dot_nn(live_bits, order)[:1] > 0.5
    for copies in forwards[1:]:
        for copy in copies:
            copy.wait_recv()
    exchanged(srow, rx, aa_s.at[0], aa_r.at[0])

    rows = rx[...].reshape(64, D)
    col_normed = normalize(rows, 1)
    own_rows = pl.ds(pl.multiple_of(64 * c, 64), 64)
    kf[own_rows, :] = dot_nt(col_normed, wfull[1]).astype(BF16)
    vf_copies = []
    kcopy = remote(kf.at[own_rows, :], kf.at[own_rows, :], kv_s.at[0], kv_r.at[0], sibling)
    kcopy.start()
    vf[own_rows, :] = dot_nt(col_normed, wfull[2]).astype(BF16)
    vcopy = remote(vf.at[own_rows, :], vf.at[own_rows, :], kv_s.at[1], kv_r.at[1], sibling)
    vcopy.start()
    col_queries = rounded(dot_nt(col_normed, wfull[3]))
    kcopy.wait_recv()
    vcopy.wait_recv()
    low = lax.broadcasted_iota(jnp.int32, (64, 128), 1) < HEAD
    col_context = []
    for p in range(6):
        cols = slice(128 * p, 128 * p + 128)
        pair = col_queries[:, cols]
        stacked = jnp.concatenate([jnp.where(low, pair, 0.0), jnp.where(low, 0.0, pair)], axis=0).astype(BF16)
        col_probs = softmax(dot_nt(stacked, kf[:, cols]) * COL_SCALE, seq_keys)
        result = dot_nn(col_probs, vf[:, cols])
        col_context.append(jnp.where(low, result[:64], result[64:]))
    col_context = jnp.concatenate(col_context, axis=1).astype(BF16)
    final = rows + dot_nt(col_context, wfull[4])
    for i in range(4):
        xb[i] = final[:, PART * i : PART * i + PART].astype(BF16)

    returns = {}
    for k in (2, 1, 3):
        other = (x + k) % 4
        returns[k] = remote(xb.at[other], xr.at[x], ox_s.at[k - 1], ox_r.at[k - 1], dev(z, y, c, other))
        returns[k].start()
    xr[x] = xb[x]
    for k in (1, 3, 2):
        returns[k].wait_recv()
    mrow[...] = jnp.concatenate([xr[i].astype(F32) for i in range(4)], axis=1).reshape(64, 1, D)
    exchange(mrow, mrx, bb_s.at[0], bb_r.at[0])

    for copies in (gathers, scatters, spreads, probs, returns):
        for copy in copies.values():
            copy.wait_send()
    for copies in wgather + forwards + [swaps, [kcopy, vcopy]]:
        for copy in copies:
            copy.wait_send()
    for here, copy in contexts:
        if here is None:
            copy.wait_send()
        else:

            @pl.when(jnp.logical_not(here))
            def _():
                copy.wait_send()

    exchanged(mrow, mrx, bb_s.at[0], bb_r.at[0])
    placed = mrx[...].reshape(64, D)
    out[0] = jnp.concatenate(
        [placed[:, PART * i : PART * i + PART].T for i in range(4)], axis=1
    ).astype(BF16)


def shards(
    alignment,
    row_query_key,
    row_value,
    row_output,
    col_query_key,
    col_value,
    col_output,
    sequence_mask,
    residue_mask,
):
    dma = pltpu.SemaphoreType.DMA
    in_hbm = pl.BlockSpec(memory_space=pl.ANY)
    in_vmem = pl.BlockSpec(memory_space=pltpu.VMEM)
    return pl.pallas_call(
        layer,
        out_shape=jax.ShapeDtypeStruct((1, PART, L), BF16),
        in_specs=[in_hbm] * 7 + [in_vmem] * 2,
        out_specs=in_vmem,
        scratch_shapes=[
            pltpu.VMEM((4, PART, L), BF16),
            pltpu.VMEM((3, PART, D), BF16),
            pltpu.VMEM((5, D, D), BF16),
            pltpu.VMEM((2, PART, 128), BF16),
            pltpu.VMEM((PART, L), BF16),
            pltpu.VMEM((PART, L), BF16),
            pltpu.VMEM((PART, 128), BF16),
            pltpu.VMEM((PART, L), BF16),
            pltpu.VMEM((PART, L), BF16),
            pltpu.VMEM((384, L), F32),
            pltpu.VMEM((384, L), BF16),
            pltpu.VMEM((7, 48, L), BF16),
            pltpu.VMEM((48, L), BF16),
            pltpu.VMEM((7, 48, L), BF16),
            pltpu.VMEM((384, L), BF16),
            pltpu.VMEM((2, 128, PART), BF16),
            pltpu.VMEM((4, 64, PART), BF16),
            pltpu.VMEM((64, 1, D), F32),
            pltpu.VMEM((64, 1, D), F32),
            pltpu.VMEM((SEQS, D), BF16),
            pltpu.VMEM((SEQS, D), BF16),
            pltpu.VMEM((4, 64, PART), BF16),
            pltpu.VMEM((4, 64, PART), BF16),
            pltpu.VMEM((64, 1, D), F32),
            pltpu.VMEM((64, 1, D), F32),
            dma((9,)),
            dma((3,)), dma((3,)),
            dma((5, 3)), dma((5, 3)),
            dma((5, 3)), dma((5, 3)),
            dma((3,)), dma((3,)),
            dma((7,)), dma((7,)),
            dma((7,)), dma((7,)),
            dma((7,)), dma((7,)),
            dma((4,)), dma((4,)),
            dma((1,)), dma((1,)),
            dma((2,)), dma((2,)),
            dma((3,)), dma((3,)),
            dma((1,)), dma((1,)),
        ],
        compiler_params=pltpu.CompilerParams(
            collective_id=0, has_side_effects=True, vmem_limit_bytes=40 << 20
        ),
        name="layer",
    )(
        alignment,
        row_query_key,
        row_value,
        row_output,
        col_query_key,
        col_value,
        col_output,
        sequence_mask.reshape(1, SEQS),
        residue_mask.reshape(1, L),
    )


def solution(mesh):
    placed = (
        P("seq", "head", None),
        P(None, "head", None),
        P("head", None),
        P("head", None),
        P(None, "head", None),
        P("head", None),
        P("head", None),
        P(),
        P(),
    )
    return jax.shard_map(
        shards, mesh=mesh, in_specs=placed, out_specs=P("seq", "head", None), check_vma=False
    )
```

```python
import math

import jax
import jax.numpy as jnp
from jax import lax
from jax.experimental import pallas as pl
from jax.experimental.pallas import tpu as pltpu
from jax.sharding import PartitionSpec as P

D = 768
HEADS = 12
L = 256
SEQS = 128
HEAD = D // HEADS
PART = D // 4
EPSILON = 1e-05
MASKED = -1e30
ROW_SCALE = HEAD**-0.5 / math.sqrt(SEQS)
COL_SCALE = HEAD**-0.5
MESH = pl.DeviceIdType.MESH
BF16 = jnp.bfloat16
F32 = jnp.float32


def dot_nt(a, b):
    return lax.dot_general(a, b, (((1,), (1,)), ((), ())), preferred_element_type=F32)


def dot_nn(a, b):
    return lax.dot_general(a, b, (((1,), (0,)), ((), ())), preferred_element_type=F32)


def dot_tn(a, b):
    return lax.dot_general(a, b, (((0,), (0,)), ((), ())), preferred_element_type=F32)


def normalize(values, axis):
    centred = values - jnp.mean(values, axis=axis, keepdims=True)
    variance = jnp.mean(centred * centred, axis=axis, keepdims=True)
    return (centred * lax.rsqrt(variance + EPSILON)).astype(BF16)


def softmax(logits, live):
    logits = jnp.where(live, logits, MASKED)
    weights = jnp.exp(logits - jnp.max(logits, axis=-1, keepdims=True))
    return (weights / jnp.sum(weights, axis=-1, keepdims=True)).astype(BF16)


def rounded(values):
    return values.astype(BF16).astype(F32)


def layer(
    al, rqk, rv, ro, cqk, cv, co, smask, rmask, out,
    ag, wrow, wfull, qh, kk, vv, qrx, krx, vrx, pacc, pb, ra, sb, rb, pf,
    ctxb, cx, srow, rx, kf, vf, xb, xr, mrow, mrx,
    lsem, xs_s, xs_r, wg_s, wg_r, wf_s, wf_r, co_s, co_r, ra_s, ra_r, rb_s, rb_r,
    pa_s, pa_r, cx_s, cx_r, aa_s, aa_r, kv_s, kv_r, ox_s, ox_r, bb_s, bb_r,
):
    s = lax.axis_index("seq")
    x = lax.axis_index("head")
    z, y, c = s // 16, (s // 2) % 8, s % 2
    zy = z * 8 + y
    first = c == 0
    ia = jnp.where(first, y, z)
    ib = jnp.where(first, z, y)

    def dev(z_, y_, c_, x_):
        return (z_ * 16 + y_ * 2 + c_, x_)

    def dev_a(g):
        return dev(jnp.where(first, z, g), jnp.where(first, g, y), c, x)

    def dev_b(g):
        return dev(jnp.where(first, g, z), jnp.where(first, y, g), c, x)

    def remote(src, dst, ss, rs, target):
        return pltpu.make_async_remote_copy(
            src_ref=src, dst_ref=dst, send_sem=ss, recv_sem=rs, device_id=target, device_id_type=MESH
        )

    sibling = dev(z, y, 1 - c, x)

    mine = pl.ds(pl.multiple_of(PART * x, 64), PART)
    weights = (ro, cqk.at[1], cv, cqk.at[0], co)
    loads = [pltpu.make_async_copy(al.at[0], ag.at[x], lsem.at[0])]
    for i, ref in enumerate((rqk.at[0], rqk.at[1], rv)):
        loads.append(pltpu.make_async_copy(ref, wrow.at[i], lsem.at[1 + i]))
    for i, ref in enumerate(weights):
        loads.append(pltpu.make_async_copy(ref, wfull.at[i, mine, :], lsem.at[4 + i]))
    for copy in loads:
        copy.start()

    barrier = pltpu.get_barrier_semaphore()
    greeted = [dev_a((ia + k) % 8) for k in range(1, 8)] + [dev_b((ib + k) % 8) for k in range(1, 8)]
    greeted += [dev(z, y, (c + j) % 2, (x + k) % 4) for k in range(4) for j in range(2) if j or k]
    for target in greeted:
        pl.semaphore_signal(barrier, inc=1, device_id=target, device_id_type=MESH)
    loads[0].wait()
    pl.semaphore_wait(barrier, len(greeted))

    for j in range(4):
        for k in (2, 1, 3):
            part = ag.at[x, 48 * j : 48 * j + 48, :]
            remote(part, part, xs_s.at[k - 1], xs_r.at[k - 1], dev(z, y, c, (x + k) % 4)).start()
    for copy in loads[1:]:
        copy.wait()
    for k in (1, 3, 2):
        pltpu.make_async_copy(ag.at[0], ag.at[0], xs_r.at[k - 1]).wait()

    floats = ag[...].reshape(D, L).astype(F32)
    normed = normalize(floats, 0)
    live = jnp.sum(
        jnp.where(lax.broadcasted_iota(jnp.int32, (1, SEQS), 1) == s, smask[...], 0), axis=-1, keepdims=True
    ).astype(F32)
    keys = dot_nn(wrow[1], normed).astype(BF16)
    kk[...] = keys
    queries = (dot_nn(wrow[0], normed) * live).astype(BF16)
    qh[0] = queries[:, :128]
    qh[1] = queries[:, 128:]
    swaps = [
        remote(kk, krx, co_s.at[0], co_r.at[0], sibling),
        remote(qh.at[1 - c], qrx, co_s.at[1], co_r.at[1], sibling),
        remote(vv, vrx, co_s.at[2], co_r.at[2], sibling),
    ]
    swaps[0].start()
    swaps[1].start()
    vv[...] = dot_nn(wrow[2], normed).astype(BF16)
    swaps[2].start()

    own_q = qh[c]
    for h in range(3):
        r = slice(HEAD * h, HEAD * h + HEAD)
        pacc[128 * h : 128 * h + 128, :] = dot_tn(own_q[r], keys[r])
    swaps[0].wait_recv()
    swaps[1].wait_recv()
    for h in range(3):
        r = slice(HEAD * h, HEAD * h + HEAD)
        total = pacc[128 * h : 128 * h + 128, :] + dot_tn(qrx[r, :], krx[r, :])
        pacc[128 * h : 128 * h + 128, :] = total
        pb[128 * h : 128 * h + 128, :] = total.astype(BF16)

    def chunk(g):
        return pl.ds(pl.multiple_of(48 * g, 16), 48)

    scatters = {}
    for k in (4, 3, 5, 2, 6, 1, 7):
        g = (ia + k) % 8
        scatters[k] = remote(pb.at[chunk(g), :], ra.at[k - 1], ra_s.at[k - 1], ra_r.at[k - 1], dev_a(g))
        scatters[k].start()

    def gather_weights(step, carry):
        i, j = step // 3, step % 3
        part = wfull.at[i, pl.ds(pl.multiple_of(PART * x + 96 * c + 32 * j, 32), 32), :]
        for k in (2, 1, 3):
            remote(part, part, wg_s.at[i], wg_r.at[i], dev(z, y, c, (x + k) % 4)).start()
        return carry

    lax.fori_loop(0, 9, gather_weights, 0)

    def three_halves(i, sem):
        part = wfull.at[i, :288, :]
        return pltpu.make_async_copy(part, part, sem.at[i])

    def forward(i):
        three_halves(i, wg_r).wait()
        for k in (1, 2, 3):
            rows = pl.ds(pl.multiple_of(PART * ((x + 4 - k) % 4) + 96 * c, 32), 96)
            part = wfull.at[i, rows, :]
            remote(part, part, wf_s.at[i], wf_r.at[i], sibling).start()

    for k in (1, 7, 2, 6, 3, 5, 4):
        scatters[k].wait_recv()
    summed = pacc[pl.ds(pl.multiple_of(48 * ia, 16), 48), :]
    for k in range(7):
        summed = summed + ra[k].astype(F32)
    sb[...] = summed.astype(BF16)
    spreads = {}
    for k in (4, 3, 5, 2, 6, 1, 7):
        spreads[k] = remote(sb, rb.at[k - 1], rb_s.at[k - 1], rb_r.at[k - 1], dev_b((ib + k) % 8))
        spreads[k].start()
    pick = (
        lax.broadcasted_iota(jnp.int32, (64, L), 1) == lax.broadcasted_iota(jnp.int32, (64, L), 0) + 64 * x
    ).astype(BF16)
    quarter = jnp.concatenate([dot_nt(pick, ag[i]) for i in range(4)], axis=1)
    for k in (1, 7, 2, 6, 3, 5, 4):
        spreads[k].wait_recv()
    for k in range(7):
        summed = summed + rb[k].astype(F32)
    own_chunk = chunk(ia)
    pf[own_chunk, :] = softmax(summed * ROW_SCALE, rmask[...] > 0)
    probs = {}
    for k in (4, 3, 5, 2, 6, 1, 7):
        probs[k] = remote(
            pf.at[own_chunk, :], pf.at[own_chunk, :], pa_s.at[k - 1], pa_r.at[k - 1], dev_a((ia + k) % 8)
        )
        probs[k].start()
    forward(0)
    swaps[2].wait_recv()
    for k in (1, 7, 2, 6, 3, 5, 4):
        probs[k].wait_recv()

    mixed = []
    for h in range(3):
        r = slice(HEAD * h, HEAD * h + HEAD)
        both = jnp.concatenate([vv[r, :], vrx[r, :]], axis=0)
        mixed.append(dot_nt(pf[128 * h : 128 * h + 128, :], both))
    ctxb[0] = jnp.concatenate([m[:, :HEAD] for m in mixed], axis=1).astype(BF16)
    ctxb[1] = jnp.concatenate([m[:, HEAD:] for m in mixed], axis=1).astype(BF16)
    contexts = []
    for j in range(2):
        for q in range(2):
            src = ctxb.at[j, 64 * q : 64 * q + 64, :]
            owner = 2 * c + q
            copy = remote(src, cx.at[x], cx_s.at[2 * j + q], cx_r.at[x], dev(z, y, (c + j) % 2, owner))
            if j:
                copy.start()
                contexts.append((None, copy))
            else:
                here = owner == x

                @pl.when(here)
                def _():
                    pltpu.make_async_copy(src, cx.at[x], cx_r.at[x]).start()

                @pl.when(jnp.logical_not(here))
                def _():
                    copy.start()

                contexts.append((here, copy))
    three_halves(0, wf_r).wait()
    for i in range(4):
        pltpu.make_async_copy(ctxb.at[0, :64, :], cx.at[i], cx_r.at[i]).wait()
    context = jnp.concatenate([cx[i].astype(F32) for i in range(4)], axis=1).astype(BF16)
    stream = rounded(quarter + dot_nt(context, wfull[0]))
    srow[...] = stream.reshape(64, 1, D)

    def exchange(src, dst, ss, rs):
        def send(step, carry):
            k = (step + 36) % 64
            z_, y_ = (z + k // 8) % 8, (y + k) % 8

            @pl.when(k != 0)
            def _():
                remote(src.at[z_ * 8 + y_], dst.at[zy], ss, rs, dev(z_, y_, c, x)).start()

            return carry

        lax.fori_loop(0, 64, send, 0)
        pltpu.make_async_copy(src.at[zy], dst.at[zy], rs).start()

    def exchanged(src, dst, ss, rs):
        pltpu.make_async_copy(src, dst, rs).wait()
        pltpu.make_async_copy(src.at[:63], dst.at[:63], ss).wait()

    exchange(srow, rx, aa_s.at[0], aa_r.at[0])
    lax.fori_loop(9, 15, gather_weights, 0)
    forward(1)
    forward(2)
    order = (
        lax.broadcasted_iota(jnp.int32, (SEQS, SEQS), 0)
        == (lax.broadcasted_iota(jnp.int32, (SEQS, SEQS), 1) % 64) * 2
        + lax.broadcasted_iota(jnp.int32, (SEQS, SEQS), 1) // 64
    ).astype(BF16)
    live_bits = jnp.broadcast_to((smask[...] > 0).astype(BF16), (16, SEQS))
    seq_keys = dot_nn(live_bits, order)[:1] > 0.5
    three_halves(1, wf_r).wait()
    three_halves(2, wf_r).wait()
    exchanged(srow, rx, aa_s.at[0], aa_r.at[0])

    rows = rx[...].reshape(64, D)
    col_normed = normalize(rows, 1)
    own_rows = pl.ds(pl.multiple_of(64 * c, 64), 64)
    kf[own_rows, :] = dot_nt(col_normed, wfull[1]).astype(BF16)
    kcopy = remote(kf.at[own_rows, :], kf.at[own_rows, :], kv_s.at[0], kv_r.at[0], sibling)
    kcopy.start()
    vf[own_rows, :] = dot_nt(col_normed, wfull[2]).astype(BF16)
    vcopy = remote(vf.at[own_rows, :], vf.at[own_rows, :], kv_s.at[1], kv_r.at[1], sibling)
    vcopy.start()
    forward(3)
    forward(4)
    three_halves(3, wf_r).wait()
    col_queries = rounded(dot_nt(col_normed, wfull[3]))
    kcopy.wait_recv()
    vcopy.wait_recv()
    low = lax.broadcasted_iota(jnp.int32, (64, 128), 1) < HEAD
    col_context = []
    for p in range(6):
        cols = slice(128 * p, 128 * p + 128)
        pair = col_queries[:, cols]
        stacked = jnp.concatenate([jnp.where(low, pair, 0.0), jnp.where(low, 0.0, pair)], axis=0).astype(BF16)
        col_probs = softmax(dot_nt(stacked, kf[:, cols]) * COL_SCALE, seq_keys)
        result = dot_nn(col_probs, vf[:, cols])
        col_context.append(jnp.where(low, result[:64], result[64:]))
    col_context = jnp.concatenate(col_context, axis=1).astype(BF16)
    three_halves(4, wf_r).wait()
    final = rows + dot_nt(col_context, wfull[4])
    for i in range(4):
        xb[i] = final[:, PART * i : PART * i + PART].astype(BF16)

    returns = {}
    for k in (2, 1, 3):
        other = (x + k) % 4
        returns[k] = remote(xb.at[other], xr.at[x], ox_s.at[k - 1], ox_r.at[k - 1], dev(z, y, c, other))
        returns[k].start()
    xr[x] = xb[x]
    for k in (1, 3, 2):
        returns[k].wait_recv()
    mrow[...] = jnp.concatenate([xr[i].astype(F32) for i in range(4)], axis=1).reshape(64, 1, D)
    exchange(mrow, mrx, bb_s.at[0], bb_r.at[0])

    for k in range(3):
        pltpu.make_async_copy(ag.at[0], ag.at[0], xs_s.at[k]).wait()
    for i in range(5):
        three_halves(i, wg_s).wait()
        three_halves(i, wf_s).wait()
    for copies in (scatters, spreads, probs, returns):
        for copy in copies.values():
            copy.wait_send()
    for copy in swaps + [kcopy, vcopy]:
        copy.wait_send()
    for here, copy in contexts:
        if here is None:
            copy.wait_send()
        else:

            @pl.when(jnp.logical_not(here))
            def _():
                copy.wait_send()

    exchanged(mrow, mrx, bb_s.at[0], bb_r.at[0])
    placed = mrx[...].reshape(64, D)
    out[0] = jnp.concatenate(
        [placed[:, PART * i : PART * i + PART].T for i in range(4)], axis=1
    ).astype(BF16)


def shards(
    alignment,
    row_query_key,
    row_value,
    row_output,
    col_query_key,
    col_value,
    col_output,
    sequence_mask,
    residue_mask,
):
    dma = pltpu.SemaphoreType.DMA
    in_hbm = pl.BlockSpec(memory_space=pltpu.HBM)
    in_vmem = pl.BlockSpec(memory_space=pltpu.VMEM)
    return pl.pallas_call(
        layer,
        out_shape=jax.ShapeDtypeStruct((1, PART, L), BF16),
        in_specs=[in_hbm] * 7 + [in_vmem] * 2,
        out_specs=in_vmem,
        scratch_shapes=[
            pltpu.VMEM((4, PART, L), BF16),
            pltpu.VMEM((3, PART, D), BF16),
            pltpu.VMEM((5, D, D), BF16),
            pltpu.VMEM((2, PART, 128), BF16),
            pltpu.VMEM((PART, L), BF16),
            pltpu.VMEM((PART, L), BF16),
            pltpu.VMEM((PART, 128), BF16),
            pltpu.VMEM((PART, L), BF16),
            pltpu.VMEM((PART, L), BF16),
            pltpu.VMEM((384, L), F32),
            pltpu.VMEM((384, L), BF16),
            pltpu.VMEM((7, 48, L), BF16),
            pltpu.VMEM((48, L), BF16),
            pltpu.VMEM((7, 48, L), BF16),
            pltpu.VMEM((384, L), BF16),
            pltpu.VMEM((2, 128, PART), BF16),
            pltpu.VMEM((4, 64, PART), BF16),
            pltpu.VMEM((64, 1, D), F32),
            pltpu.VMEM((64, 1, D), F32),
            pltpu.VMEM((SEQS, D), BF16),
            pltpu.VMEM((SEQS, D), BF16),
            pltpu.VMEM((4, 64, PART), BF16),
            pltpu.VMEM((4, 64, PART), BF16),
            pltpu.VMEM((64, 1, D), F32),
            pltpu.VMEM((64, 1, D), F32),
            dma((9,)),
            dma((3,)), dma((3,)),
            dma((5,)), dma((5,)),
            dma((5,)), dma((5,)),
            dma((3,)), dma((3,)),
            dma((7,)), dma((7,)),
            dma((7,)), dma((7,)),
            dma((7,)), dma((7,)),
            dma((4,)), dma((4,)),
            dma((1,)), dma((1,)),
            dma((2,)), dma((2,)),
            dma((3,)), dma((3,)),
            dma((1,)), dma((1,)),
        ],
        compiler_params=pltpu.CompilerParams(
            collective_id=0, has_side_effects=True, vmem_limit_bytes=60 << 20
        ),
        name="layer",
    )(
        alignment,
        row_query_key,
        row_value,
        row_output,
        col_query_key,
        col_value,
        col_output,
        sequence_mask.reshape(1, SEQS),
        residue_mask.reshape(1, L),
    )


def solution(mesh):
    placed = (
        P("seq", "head", None),
        P(None, "head", None),
        P("head", None),
        P("head", None),
        P(None, "head", None),
        P("head", None),
        P("head", None),
        P(),
        P(),
    )
    return jax.shard_map(
        shards, mesh=mesh, in_specs=placed, out_specs=P("seq", "head", None), check_vma=False
    )
```

```python
import math

import jax
import jax.numpy as jnp
from jax import lax
from jax.experimental import pallas as pl
from jax.experimental.pallas import tpu as pltpu
from jax.sharding import PartitionSpec as P

D = 768
HEADS = 12
L = 256
SEQS = 128
HEAD = D // HEADS
PART = D // 4
EPSILON = 1e-05
MASKED = -1e30
ROW_SCALE = HEAD**-0.5 / math.sqrt(SEQS)
COL_SCALE = HEAD**-0.5
MESH = pl.DeviceIdType.MESH
BF16 = jnp.bfloat16
F32 = jnp.float32
FAR = (4, 3, 5, 2, 6, 1, 7)
NEAR = FAR[::-1]
BOTH_FAR = sorted(((a, b) for a in range(8) for b in range(8)), key=lambda d: -min(d[0], 8 - d[0]) - min(d[1], 8 - d[1]))


def dot_nt(a, b):
    return lax.dot_general(a, b, (((1,), (1,)), ((), ())), preferred_element_type=F32)


def dot_nn(a, b):
    return lax.dot_general(a, b, (((1,), (0,)), ((), ())), preferred_element_type=F32)


def dot_tn(a, b):
    return lax.dot_general(a, b, (((0,), (0,)), ((), ())), preferred_element_type=F32)


def normalize(values, axis):
    centred = values - jnp.mean(values, axis=axis, keepdims=True)
    variance = jnp.mean(centred * centred, axis=axis, keepdims=True)
    return (centred * lax.rsqrt(variance + EPSILON)).astype(BF16)


def softmax(logits, live):
    logits = jnp.where(live, logits, MASKED)
    weights = jnp.exp(logits - jnp.max(logits, axis=-1, keepdims=True))
    return (weights / jnp.sum(weights, axis=-1, keepdims=True)).astype(BF16)


def rounded(values):
    return values.astype(BF16).astype(F32)


def layer(
    al, rqk, rv, ro, cqk, cv, co, smask, rmask, out,
    ag, wrow, wfull, qh, kk, vall, qrx, krx, pown, pacc, pb, ra, sb, rb, pp,
    msg, rxc, srow, arx, kf, vf, xb, xr, mrow, mrx,
    lsem, met, xs_s, xs_r, wg_s, wg_r, wf_s, wf_r, co_s, co_r, ra_s, ra_r, rb_s, rb_r,
    vg_s, vg_r, pr_s, pr_r, cx_s, cx_r, aa_s, aa_r, kv_s, kv_r, ox_s, ox_r, bb_s, bb_r,
):
    s = lax.axis_index("seq")
    x = lax.axis_index("head")
    z, y, c = s >> 4, (s >> 1) & 7, s & 1
    first = c == 0
    ia = jnp.where(first, y, z)
    ib = jnp.where(first, z, y)
    odd = ia & 1
    sign = 2 * odd - 1
    half = x >> 1
    own_a = jnp.where(half == 0, y, z)
    own_b = jnp.where(half == 0, z, y)
    own_n = own_a * 8 + own_b
    even_a = own_a & 6
    home = (own_a & 1) == c
    a_step = jnp.where(half == 0, 2, 16)
    b_step = jnp.where(half == 0, 16, 2)

    def dev(z_, y_, c_, x_):
        return (z_ * 16 + y_ * 2 + c_, x_)

    def dev_a(g):
        return dev(jnp.where(first, z, g), jnp.where(first, g, y), c, x)

    def dev_b(g):
        return dev(jnp.where(first, g, z), jnp.where(first, y, g), c, x)

    def remote(src, dst, ss, rs, target):
        return pltpu.make_async_remote_copy(
            src_ref=src, dst_ref=dst, send_sem=ss, recv_sem=rs, device_id=target, device_id_type=MESH
        )

    def bytes_of(ref, sem):
        return pltpu.make_async_copy(ref, ref, sem)

    def to_device(here, src, dst, ss, rs, target):
        if here is None:
            remote(src, dst, ss, rs, target).start()
            return

        @pl.when(here)
        def _():
            pltpu.make_async_copy(src, dst, rs).start()

        @pl.when(jnp.logical_not(here))
        def _():
            remote(src, dst, ss, rs, target).start()

    def wait_rows_sent(ref, count, one_stays, sem):
        @pl.when(one_stays)
        def _():
            bytes_of(ref.at[: count - 1], sem).wait()

        @pl.when(jnp.logical_not(one_stays))
        def _():
            bytes_of(ref, sem).wait()

    sibling = dev(z, y, 1 - c, x)

    barrier = pltpu.get_barrier_semaphore()
    ring = [dev_a((ia + k) & 7) for k in FAR] + [dev_b((ib + k) & 7) for k in FAR]
    greeted = ring + [dev(z, y, c ^ j, (x + k) & 3) for k in range(4) for j in range(2) if j or k]
    loads = [pltpu.make_async_copy(al.at[0], ag.at[x], lsem.at[0])]
    loads[0].start()
    for target in greeted:
        pl.semaphore_signal(barrier, inc=1, device_id=target, device_id_type=MESH)
    mine = pl.ds(pl.multiple_of(PART * x, 64), PART)
    weights = (ro, cqk.at[1], cv, cqk.at[0], co)
    for i, ref in enumerate((rqk.at[0], rqk.at[1], rv)):
        loads.append(pltpu.make_async_copy(ref, wrow.at[i], lsem.at[1 + i]))
    for i, ref in enumerate(weights):
        loads.append(pltpu.make_async_copy(ref, wfull.at[i, mine, :], lsem.at[4 + i]))
    for copy in loads[1:]:
        copy.start()
    loads[0].wait()
    pl.semaphore_wait(barrier, len(greeted))

    for j in range(4):
        for k in (2, 1, 3):
            part = ag.at[x, 48 * j : 48 * j + 48, :]
            remote(part, part, xs_s.at[k - 1], xs_r.at[k - 1], dev(z, y, c, (x + k) & 3)).start()
    for target in ring:
        pl.semaphore_signal(met.at[0], inc=1, device_id=target, device_id_type=MESH)
    pl.semaphore_wait(met.at[0], len(ring))
    pl.semaphore_signal(met.at[1], inc=1, device_id=sibling, device_id_type=MESH)
    pl.semaphore_wait(met.at[1], 1)
    for copy in loads[1:]:
        copy.wait()
    for k in (1, 3, 2):
        bytes_of(ag.at[0], xs_r.at[k - 1]).wait()

    onward = 1 - 2 * c
    after, before = dev(z, y, c, (x + onward) & 3), dev(z, y, c, (x - onward) & 3)

    def pieces(i, owner, ss, rs, target):
        for j in range(3):
            part = wfull.at[i, pl.ds(pl.multiple_of(PART * owner + 96 * c + 32 * j, 32), 32), :]
            remote(part, part, ss, rs, target).start()

    def gather_weights(i):
        pieces(i, x, wg_s.at[i], wg_r.at[i, 0], after)
        pieces(i, x, wg_s.at[i], wg_r.at[i, 1], before)

    def relay(i):
        bytes_of(wfull.at[i, :96, :], wg_r.at[i, 0]).wait()
        pieces(i, (x - onward) & 3, wg_s.at[i], wg_r.at[i, 2], after)

    def three_halves(i, sem):
        return bytes_of(wfull.at[i, :288, :], sem.at[i])

    def forward(i):
        bytes_of(wfull.at[i, :96, :], wg_r.at[i, 1]).wait()
        bytes_of(wfull.at[i, :96, :], wg_r.at[i, 2]).wait()
        for k in (1, 2, 3):
            rows = pl.ds(pl.multiple_of(PART * ((x - k) & 3) + 96 * c, 32), 96)
            part = wfull.at[i, rows, :]
            remote(part, part, wf_s.at[i], wf_r.at[i], sibling).start()

    def send_values(p):
        for piece in range(4):
            for j in (3, 2, 1):
                rows = pl.ds(48 * piece, 48)
                g = (ia + sign * (-j if j == 2 else j)) & 7
                remote(
                    vall.at[0, p, rows, :], vall.at[j, p, rows, :], vg_s.at[0], vg_r.at[j - 1, p], dev_a(g)
                ).start()

    floats = ag[...].reshape(D, L).astype(F32)
    normed = normalize(floats, 0)
    live = jnp.sum(
        jnp.where(lax.broadcasted_iota(jnp.int32, (1, SEQS), 1) == s, smask[...], 0), axis=-1, keepdims=True
    ).astype(F32)
    swaps = [
        remote(kk, krx, co_s.at[0], co_r.at[0], sibling),
        remote(qh.at[1 - c], qrx, co_s.at[1], co_r.at[1], sibling),
        remote(vall.at[0, c], vall.at[0, c], co_s.at[2], co_r.at[2], sibling),
    ]
    vall[0, c] = dot_nn(wrow[2], normed).astype(BF16)
    swaps[2].start()
    send_values(c)
    keys = dot_nn(wrow[1], normed).astype(BF16)
    kk[...] = keys
    swaps[0].start()
    queries = (dot_nn(wrow[0], normed) * live).astype(BF16)
    qh[0] = queries[:, :128]
    qh[1] = queries[:, 128:]
    swaps[1].start()
    for i in (0, 1):
        gather_weights(i)

    own_q = qh[c]
    for h in range(3):
        r = slice(HEAD * h, HEAD * h + HEAD)
        pown[128 * h : 128 * h + 128, :] = dot_tn(own_q[r], keys[r])
    swaps[0].wait_recv()
    swaps[1].wait_recv()
    for h in range(3):
        r = slice(HEAD * h, HEAD * h + HEAD)
        total = pown[128 * h : 128 * h + 128, :] + dot_tn(qrx[r, :], krx[r, :])
        for g in range(8):
            piece = total[16 * g : 16 * g + 16]
            pacc[g, 16 * h : 16 * h + 16, :] = piece
            pb[g, 16 * h : 16 * h + 16, :] = piece.astype(BF16)

    scatters = {}
    for k in FAR:
        g = (ia + k) & 7
        scatters[k] = remote(pb.at[g], ra.at[k - 1], ra_s.at[k - 1], ra_r.at[k - 1], dev_a(g))
        scatters[k].start()

    swaps[2].wait_recv()
    send_values(1 - c)

    for i in (2, 3):
        gather_weights(i)

    pick = (
        lax.broadcasted_iota(jnp.int32, (64, L), 1)
        == 2 * lax.broadcasted_iota(jnp.int32, (64, L), 0) + (128 * half + (x & 1))
    ).astype(BF16)
    srow[...] = jnp.concatenate([dot_nt(pick, ag[i]) for i in range(4)], axis=1).reshape(64, 1, D)

    for k in NEAR:
        scatters[k].wait_recv()
    summed = pacc[ia]
    for k in range(7):
        summed = summed + ra[k].astype(F32)
    sb[...] = summed.astype(BF16)
    spreads = {}
    for k in FAR:
        spreads[k] = remote(sb, rb.at[k - 1], rb_s.at[k - 1], rb_r.at[k - 1], dev_b((ib + k) & 7))
        spreads[k].start()

    for i in range(4):
        relay(i)
    for da, db in BOTH_FAR:
        a, b = (own_a + da) & 7, (own_b + db) & 7
        d = (own_a - (a & 6)) & 7
        low = jnp.logical_or(d == 0, d >= 5)
        core = jnp.where(low, 0, 1)
        j = jnp.where(low, (8 - d) & 7, d - 1)
        to_device(
            home if da == db == 0 else None,
            srow.at[a * 8 + b], arx.at[(2 * j + c) * 8 + own_b], aa_s.at[0], aa_r.at[0],
            (a * a_step + b * b_step + core, x),
        )
    for k in NEAR:
        spreads[k].wait_recv()
    for k in range(7):
        summed = summed + rb[k].astype(F32)
    pp[odd] = softmax(summed * ROW_SCALE, rmask[...] > 0)
    paired = remote(pp.at[odd], pp.at[odd], pr_s.at[0], pr_r.at[0], dev_a(ia ^ 1))
    paired.start()
    for j in (1, 2, 3):
        for p in range(2):
            bytes_of(vall.at[j, p], vg_r.at[j - 1, p]).wait()

    def context_to_owners(parity, g, own):
        parts = []
        for h in range(3):
            r = slice(HEAD * h, HEAD * h + HEAD)
            values = jnp.concatenate([vall[j, p, r, :] for j in range(4) for p in range(2)], axis=0)
            parts.append(rounded(dot_nt(pp[parity, 16 * h : 16 * h + 16, :], values)))
        msg[pl.ds(16 * parity, 16)] = jnp.concatenate(parts, axis=1).reshape(16, 1, 2 * D)

        for db in (4, 3, 5, 2, 6, 1, 7, 0):
            b = (ib + db) & 7
            z_, y_ = jnp.where(first, b, g), jnp.where(first, g, b)
            for q in range(2):
                stays = jnp.logical_and(2 * c + q == x, odd == c) if own and db == 0 else None
                to_device(
                    stays, msg.at[16 * parity + 2 * b + q], rxc.at[x * 8 + ib], cx_s.at[0], cx_r.at[0],
                    dev(z_, y_, odd, 2 * c + q),
                )

    context_to_owners(odd, ia, True)
    paired.wait_recv()
    context_to_owners(1 - odd, ia ^ 1, False)

    gather_weights(4)
    for i in range(4):
        forward(i)
    t = lax.broadcasted_iota(jnp.int32, (SEQS, SEQS), 1)
    core_t, j_t, p_t, b_t = t >> 6, (t >> 4) & 3, (t >> 3) & 1, t & 7
    a_t = (even_a + core_t + (2 * core_t - 1) * j_t) & 7
    seq_t = jnp.where(half == 0, b_t * 16 + a_t * 2, a_t * 16 + b_t * 2) + p_t
    order = (lax.broadcasted_iota(jnp.int32, (SEQS, SEQS), 0) == seq_t).astype(BF16)
    live_bits = jnp.broadcast_to((smask[...] > 0).astype(BF16), (16, SEQS))
    seq_keys = dot_nn(live_bits, order)[:1] > 0.5
    bytes_of(arx, aa_r.at[0]).wait()
    for i in range(4):
        three_halves(i, wf_r).wait()
    bytes_of(rxc, cx_r.at[0]).wait()

    arrived = rxc[...].reshape(32, 2 * D)
    context = jnp.concatenate(
        [
            jnp.concatenate(
                [
                    arrived[8 * i : 8 * i + 8, 512 * h + HEAD * jp : 512 * h + HEAD * jp + HEAD]
                    for i in range(4)
                    for h in range(3)
                ],
                axis=1,
            )
            for jp in range(8)
        ],
        axis=0,
    ).astype(BF16)
    rows = rounded(arx[...].reshape(64, D) + dot_nt(context, wfull[0]))
    col_normed = normalize(rows, 1)
    own_rows = pl.ds(pl.multiple_of(64 * c, 64), 64)
    kf[own_rows, :] = dot_nt(col_normed, wfull[1]).astype(BF16)
    kcopy = remote(kf.at[own_rows, :], kf.at[own_rows, :], kv_s.at[0], kv_r.at[0], sibling)
    kcopy.start()
    vf[own_rows, :] = dot_nt(col_normed, wfull[2]).astype(BF16)
    vcopy = remote(vf.at[own_rows, :], vf.at[own_rows, :], kv_s.at[1], kv_r.at[1], sibling)
    vcopy.start()
    relay(4)
    col_queries = rounded(dot_nt(col_normed, wfull[3]))
    kcopy.wait_recv()
    vcopy.wait_recv()
    low = lax.broadcasted_iota(jnp.int32, (64, 128), 1) < HEAD
    col_context = []
    for p in range(6):
        cols = slice(128 * p, 128 * p + 128)
        pair = col_queries[:, cols]
        stacked = jnp.concatenate([jnp.where(low, pair, 0.0), jnp.where(low, 0.0, pair)], axis=0).astype(BF16)
        col_probs = softmax(dot_nt(stacked, kf[:, cols]) * COL_SCALE, seq_keys)
        result = dot_nn(col_probs, vf[:, cols])
        col_context.append(jnp.where(low, result[:64], result[64:]))
    col_context = jnp.concatenate(col_context, axis=1).astype(BF16)
    forward(4)
    three_halves(4, wf_r).wait()
    mrow[...] = rounded(rows + dot_nt(col_context, wfull[4])).reshape(64, 1, D)

    for db in (4, 3, 5, 2, 6, 1, 7, 0):
        b = (own_b + db) & 7
        for j in (3, 2, 1, 0):
            a = (even_a + c + (2 * c - 1) * j) & 7
            for dp in range(2):
                p = c ^ dp
                to_device(
                    home if db == j == dp == 0 else None,
                    mrow.at[(2 * j + p) * 8 + b], mrx.at[own_n], bb_s.at[0], bb_r.at[0],
                    (a * a_step + b * b_step + p, x),
                )

    for k in range(3):
        bytes_of(ag.at[0], xs_s.at[k]).wait()
    for i in range(5):
        three_halves(i, wg_s).wait()
        three_halves(i, wf_s).wait()
    bytes_of(vall.at[1:4], vg_s.at[0]).wait()
    for copies in (scatters, spreads):
        for copy in copies.values():
            copy.wait_send()
    for copy in swaps + [paired, kcopy, vcopy]:
        copy.wait_send()
    wait_rows_sent(srow, 64, home, aa_s.at[0])
    wait_rows_sent(msg, 32, jnp.logical_and(odd == c, half == c), cx_s.at[0])

    bytes_of(mrx, bb_r.at[0]).wait()
    placed = mrx[...].reshape(64, D)
    for i in range(4):
        xb[i] = placed[:, PART * i : PART * i + PART].astype(BF16)
    returns = {}
    for k in (2, 1, 3):
        other = (x + k) & 3
        returns[k] = remote(xb.at[other], xr.at[x], ox_s.at[k - 1], ox_r.at[k - 1], dev(z, y, c, other))
        returns[k].start()
    xr[x] = xb[x]
    place = lax.broadcasted_iota(jnp.int32, (128, 128), 0)
    spread = (lax.broadcasted_iota(jnp.int32, (128, 128), 1) == 2 * (place & 63) + (place >> 6)).astype(BF16)
    wait_rows_sent(mrow, 64, home, bb_s.at[0])
    for k in (1, 3, 2):
        returns[k].wait_recv()
    for i in range(2):
        both = jnp.concatenate([xr[2 * i], xr[2 * i + 1]], axis=0)
        out[0, :, 128 * i : 128 * i + 128] = dot_tn(both, spread).astype(BF16)
    for copy in returns.values():
        copy.wait_send()


def shards(
    alignment,
    row_query_key,
    row_value,
    row_output,
    col_query_key,
    col_value,
    col_output,
    sequence_mask,
    residue_mask,
):
    dma = pltpu.SemaphoreType.DMA
    in_hbm = pl.BlockSpec(memory_space=pltpu.HBM)
    in_vmem = pl.BlockSpec(memory_space=pltpu.VMEM)
    return pl.pallas_call(
        layer,
        out_shape=jax.ShapeDtypeStruct((1, PART, L), BF16),
        in_specs=[in_hbm] * 7 + [in_vmem] * 2,
        out_specs=in_vmem,
        scratch_shapes=[
            pltpu.VMEM((4, PART, L), BF16),
            pltpu.VMEM((3, PART, D), BF16),
            pltpu.VMEM((5, D, D), BF16),
            pltpu.VMEM((2, PART, 128), BF16),
            pltpu.VMEM((PART, L), BF16),
            pltpu.VMEM((4, 2, PART, L), BF16),
            pltpu.VMEM((PART, 128), BF16),
            pltpu.VMEM((PART, L), BF16),
            pltpu.VMEM((384, L), F32),
            pltpu.VMEM((8, 48, L), F32),
            pltpu.VMEM((8, 48, L), BF16),
            pltpu.VMEM((7, 48, L), BF16),
            pltpu.VMEM((48, L), BF16),
            pltpu.VMEM((7, 48, L), BF16),
            pltpu.VMEM((2, 48, L), BF16),
            pltpu.VMEM((32, 1, 2 * D), F32),
            pltpu.VMEM((32, 1, 2 * D), F32),
            pltpu.VMEM((64, 1, D), F32),
            pltpu.VMEM((64, 1, D), F32),
            pltpu.VMEM((SEQS, D), BF16),
            pltpu.VMEM((SEQS, D), BF16),
            pltpu.VMEM((4, 64, PART), BF16),
            pltpu.VMEM((4, 64, PART), BF16),
            pltpu.VMEM((64, 1, D), F32),
            pltpu.VMEM((64, 1, D), F32),
            dma((9,)),
            pltpu.SemaphoreType.REGULAR((2,)),
            dma((3,)), dma((3,)),
            dma((5,)), dma((5, 3)),
            dma((5,)), dma((5,)),
            dma((3,)), dma((3,)),
            dma((7,)), dma((7,)),
            dma((7,)), dma((7,)),
            dma((1,)), dma((3, 2)),
            dma((1,)), dma((1,)),
            dma((1,)), dma((1,)),
            dma((1,)), dma((1,)),
            dma((2,)), dma((2,)),
            dma((3,)), dma((3,)),
            dma((1,)), dma((1,)),
        ],
        compiler_params=pltpu.CompilerParams(
            collective_id=0, has_side_effects=True, vmem_limit_bytes=60 << 20
        ),
        name="layer",
    )(
        alignment,
        row_query_key,
        row_value,
        row_output,
        col_query_key,
        col_value,
        col_output,
        sequence_mask.reshape(1, SEQS),
        residue_mask.reshape(1, L),
    )


def solution(mesh):
    placed = (
        P("seq", "head", None),
        P(None, "head", None),
        P("head", None),
        P("head", None),
        P(None, "head", None),
        P("head", None),
        P("head", None),
        P(),
        P(),
    )
    return jax.shard_map(
        shards, mesh=mesh, in_specs=placed, out_specs=P("seq", "head", None), check_vma=False
    )
```

```python
import math

import jax
import jax.numpy as jnp
from jax import lax
from jax.experimental import pallas as pl
from jax.experimental.pallas import tpu as pltpu
from jax.sharding import PartitionSpec as P

D = 768
HEADS = 12
L = 256
SEQS = 128
HEAD = D // HEADS
PART = D // 4
EPSILON = 1e-05
MASKED = -1e30
ROW_SCALE = HEAD**-0.5 / math.sqrt(SEQS)
COL_SCALE = HEAD**-0.5
MESH = pl.DeviceIdType.MESH
BF16 = jnp.bfloat16
F32 = jnp.float32
FAR = (4, 3, 5, 2, 6, 1, 7)
NEAR = FAR[::-1]
BOTH_FAR = sorted(((a, b) for a in range(8) for b in range(8)), key=lambda d: -min(d[0], 8 - d[0]) - min(d[1], 8 - d[1]))


def dot_nt(a, b):
    return lax.dot_general(a, b, (((1,), (1,)), ((), ())), preferred_element_type=F32)


def dot_nn(a, b):
    return lax.dot_general(a, b, (((1,), (0,)), ((), ())), preferred_element_type=F32)


def dot_tn(a, b):
    return lax.dot_general(a, b, (((0,), (0,)), ((), ())), preferred_element_type=F32)


def normalize(values, axis):
    centred = values - jnp.mean(values, axis=axis, keepdims=True)
    variance = jnp.mean(centred * centred, axis=axis, keepdims=True)
    return (centred * lax.rsqrt(variance + EPSILON)).astype(BF16)


def softmax(logits, live):
    logits = jnp.where(live, logits, MASKED)
    weights = jnp.exp(logits - jnp.max(logits, axis=-1, keepdims=True))
    return (weights / jnp.sum(weights, axis=-1, keepdims=True)).astype(BF16)


def rounded(values):
    return values.astype(BF16).astype(F32)


def layer(
    al, rqk, rv, ro, cqk, cv, co, smask_hbm, rmask_hbm, out,
    smask, rmask,
    ag, wrow, wfull, qh, kk, vall, qrx, krx, pown, pacc, pb, ra, sb, rb, pp,
    msg, rxc, srow, arx, kf, vf, xb, xr, mrow, mrx,
    lsem, met, xs_s, xs_r, wg_s, wg_r, wf_s, wf_r, co_s, co_r, ra_s, ra_r, rb_s, rb_r,
    vg_s, vg_r, pr_s, pr_r, cx_s, cx_r, aa_s, aa_r, kv_s, kv_r, ox_s, ox_r, bb_s, bb_r,
):
    s = lax.axis_index("seq")
    x = lax.axis_index("head")
    z, y, c = s >> 4, (s >> 1) & 7, s & 1
    first = c == 0
    ia = jnp.where(first, y, z)
    ib = jnp.where(first, z, y)
    odd = ia & 1
    sign = 2 * odd - 1
    half = x >> 1
    own_a = jnp.where(half == 0, y, z)
    own_b = jnp.where(half == 0, z, y)
    own_n = own_a * 8 + own_b
    even_a = own_a & 6
    home = (own_a & 1) == c
    a_step = jnp.where(half == 0, 2, 16)
    b_step = jnp.where(half == 0, 16, 2)

    def dev(z_, y_, c_, x_):
        return (z_ * 16 + y_ * 2 + c_, x_)

    def dev_a(g):
        return dev(jnp.where(first, z, g), jnp.where(first, g, y), c, x)

    def dev_b(g):
        return dev(jnp.where(first, g, z), jnp.where(first, y, g), c, x)

    def remote(src, dst, ss, rs, target):
        return pltpu.make_async_remote_copy(
            src_ref=src, dst_ref=dst, send_sem=ss, recv_sem=rs, device_id=target, device_id_type=MESH
        )

    def bytes_of(ref, sem):
        return pltpu.make_async_copy(ref, ref, sem)

    def to_device(here, src, dst, ss, rs, target):
        if here is None:
            remote(src, dst, ss, rs, target).start()
            return

        @pl.when(here)
        def _():
            pltpu.make_async_copy(src, dst, rs).start()

        @pl.when(jnp.logical_not(here))
        def _():
            remote(src, dst, ss, rs, target).start()

    def wait_rows_sent(ref, count, one_stays, sem):
        @pl.when(one_stays)
        def _():
            bytes_of(ref.at[: count - 1], sem).wait()

        @pl.when(jnp.logical_not(one_stays))
        def _():
            bytes_of(ref, sem).wait()

    sibling = dev(z, y, 1 - c, x)

    barrier = pltpu.get_barrier_semaphore()
    ring = [dev_a((ia + k) & 7) for k in FAR] + [dev_b((ib + k) & 7) for k in FAR]
    greeted = ring + [dev(z, y, c ^ j, (x + k) & 3) for k in range(4) for j in range(2) if j or k]
    loads = [pltpu.make_async_copy(al.at[0], ag.at[x], lsem.at[0])]
    loads[0].start()
    for target in greeted:
        pl.semaphore_signal(barrier, inc=1, device_id=target, device_id_type=MESH)
    mine = pl.ds(pl.multiple_of(PART * x, 64), PART)
    weights = (ro, cqk.at[1], cv, cqk.at[0], co)
    for i, ref in enumerate((rqk.at[0], rqk.at[1], rv)):
        loads.append(pltpu.make_async_copy(ref, wrow.at[i], lsem.at[1 + i]))
    for i, ref in enumerate(weights):
        loads.append(pltpu.make_async_copy(ref, wfull.at[i, mine, :], lsem.at[4 + i]))
    loads.append(pltpu.make_async_copy(smask_hbm, smask, lsem.at[9]))
    loads.append(pltpu.make_async_copy(rmask_hbm, rmask, lsem.at[10]))
    for copy in loads[1:]:
        copy.start()
    loads[0].wait()
    pl.semaphore_wait(barrier, len(greeted))

    for j in range(4):
        for k in (2, 1, 3):
            part = ag.at[x, 48 * j : 48 * j + 48, :]
            remote(part, part, xs_s.at[k - 1], xs_r.at[k - 1], dev(z, y, c, (x + k) & 3)).start()
    for target in ring:
        pl.semaphore_signal(met.at[0], inc=1, device_id=target, device_id_type=MESH)
    pl.semaphore_wait(met.at[0], len(ring))
    pl.semaphore_signal(met.at[1], inc=1, device_id=sibling, device_id_type=MESH)
    pl.semaphore_wait(met.at[1], 1)
    for copy in loads[1:]:
        copy.wait()
    for k in (1, 3, 2):
        bytes_of(ag.at[0], xs_r.at[k - 1]).wait()

    onward = 1 - 2 * c
    after, before = dev(z, y, c, (x + onward) & 3), dev(z, y, c, (x - onward) & 3)

    def pieces(i, owner, ss, rs, target):
        for j in range(3):
            part = wfull.at[i, pl.ds(pl.multiple_of(PART * owner + 96 * c + 32 * j, 32), 32), :]
            remote(part, part, ss, rs, target).start()

    def gather_weights(i):
        pieces(i, x, wg_s.at[i], wg_r.at[i, 0], after)
        pieces(i, x, wg_s.at[i], wg_r.at[i, 1], before)

    def relay(i):
        bytes_of(wfull.at[i, :96, :], wg_r.at[i, 0]).wait()
        pieces(i, (x - onward) & 3, wg_s.at[i], wg_r.at[i, 2], after)

    def three_halves(i, sem):
        return bytes_of(wfull.at[i, :288, :], sem.at[i])

    def forward(i):
        bytes_of(wfull.at[i, :96, :], wg_r.at[i, 1]).wait()
        bytes_of(wfull.at[i, :96, :], wg_r.at[i, 2]).wait()
        for k in (1, 2, 3):
            rows = pl.ds(pl.multiple_of(PART * ((x - k) & 3) + 96 * c, 32), 96)
            part = wfull.at[i, rows, :]
            remote(part, part, wf_s.at[i], wf_r.at[i], sibling).start()

    def send_values(p):
        for piece in range(4):
            for j in (3, 2, 1):
                rows = pl.ds(48 * piece, 48)
                g = (ia + sign * (-j if j == 2 else j)) & 7
                remote(
                    vall.at[0, p, rows, :], vall.at[j, p, rows, :], vg_s.at[0], vg_r.at[j - 1, p], dev_a(g)
                ).start()

    floats = ag[...].reshape(D, L).astype(F32)
    normed = normalize(floats, 0)
    live = jnp.sum(
        jnp.where(lax.broadcasted_iota(jnp.int32, (1, SEQS), 1) == s, smask[...], 0), axis=-1, keepdims=True
    ).astype(F32)
    swaps = [
        remote(kk, krx, co_s.at[0], co_r.at[0], sibling),
        remote(qh.at[1 - c], qrx, co_s.at[1], co_r.at[1], sibling),
        remote(vall.at[0, c], vall.at[0, c], co_s.at[2], co_r.at[2], sibling),
    ]
    keys = dot_nn(wrow[1], normed).astype(BF16)
    kk[...] = keys
    swaps[0].start()
    queries = (dot_nn(wrow[0], normed) * live).astype(BF16)
    qh[0] = queries[:, :128]
    qh[1] = queries[:, 128:]
    swaps[1].start()
    vall[0, c] = dot_nn(wrow[2], normed).astype(BF16)
    swaps[2].start()
    send_values(c)
    for i in (0, 1):
        gather_weights(i)

    own_q = qh[c]
    for h in range(3):
        r = slice(HEAD * h, HEAD * h + HEAD)
        pown[128 * h : 128 * h + 128, :] = dot_tn(own_q[r], keys[r])
    swaps[0].wait_recv()
    swaps[1].wait_recv()
    for h in range(3):
        r = slice(HEAD * h, HEAD * h + HEAD)
        total = pown[128 * h : 128 * h + 128, :] + dot_tn(qrx[r, :], krx[r, :])
        for g in range(8):
            piece = total[16 * g : 16 * g + 16]
            pacc[g, 16 * h : 16 * h + 16, :] = piece
            pb[g, 16 * h : 16 * h + 16, :] = piece.astype(BF16)

    scatters = {}
    for k in FAR:
        g = (ia + k) & 7
        scatters[k] = remote(pb.at[g], ra.at[k - 1], ra_s.at[k - 1], ra_r.at[k - 1], dev_a(g))
        scatters[k].start()

    swaps[2].wait_recv()
    send_values(1 - c)

    for i in (2, 3, 4):
        gather_weights(i)

    pick = (
        lax.broadcasted_iota(jnp.int32, (64, L), 1)
        == 2 * lax.broadcasted_iota(jnp.int32, (64, L), 0) + (128 * half + (x & 1))
    ).astype(BF16)
    srow[...] = jnp.concatenate([dot_nt(pick, ag[i]) for i in range(4)], axis=1).reshape(64, 1, D)

    for k in NEAR:
        scatters[k].wait_recv()
    summed = pacc[ia]
    for k in range(7):
        summed = summed + ra[k].astype(F32)
    sb[...] = summed.astype(BF16)
    spreads = {}
    for k in FAR:
        spreads[k] = remote(sb, rb.at[k - 1], rb_s.at[k - 1], rb_r.at[k - 1], dev_b((ib + k) & 7))
        spreads[k].start()

    for i in range(4):
        relay(i)
    for da, db in BOTH_FAR:
        a, b = (own_a + da) & 7, (own_b + db) & 7
        d = (own_a - (a & 6)) & 7
        low = jnp.logical_or(d == 0, d >= 5)
        core = jnp.where(low, 0, 1)
        j = jnp.where(low, (8 - d) & 7, d - 1)
        to_device(
            home if da == db == 0 else None,
            srow.at[a * 8 + b], arx.at[(2 * j + c) * 8 + own_b], aa_s.at[0], aa_r.at[0],
            (a * a_step + b * b_step + core, x),
        )
    for k in NEAR:
        spreads[k].wait_recv()
    for k in range(7):
        summed = summed + rb[k].astype(F32)
    pp[odd] = softmax(summed * ROW_SCALE, rmask[...] > 0)
    paired = remote(pp.at[odd], pp.at[odd], pr_s.at[0], pr_r.at[0], dev_a(ia ^ 1))
    paired.start()
    for j in (1, 2, 3):
        for p in range(2):
            bytes_of(vall.at[j, p], vg_r.at[j - 1, p]).wait()

    def context_to_owners(parity, g, own):
        parts = []
        for h in range(3):
            r = slice(HEAD * h, HEAD * h + HEAD)
            values = jnp.concatenate([vall[j, p, r, :] for j in range(4) for p in range(2)], axis=0)
            parts.append(rounded(dot_nt(pp[parity, 16 * h : 16 * h + 16, :], values)))
        msg[pl.ds(16 * parity, 16)] = jnp.concatenate(parts, axis=1).reshape(16, 1, 2 * D)

        for db in (4, 3, 5, 2, 6, 1, 7, 0):
            b = (ib + db) & 7
            z_, y_ = jnp.where(first, b, g), jnp.where(first, g, b)
            for q in range(2):
                stays = jnp.logical_and(2 * c + q == x, odd == c) if own and db == 0 else None
                to_device(
                    stays, msg.at[16 * parity + 2 * b + q], rxc.at[x * 8 + ib], cx_s.at[0], cx_r.at[0],
                    dev(z_, y_, odd, 2 * c + q),
                )

    relay(4)
    context_to_owners(odd, ia, True)
    paired.wait_recv()
    context_to_owners(1 - odd, ia ^ 1, False)

    for i in range(4):
        forward(i)
    t = lax.broadcasted_iota(jnp.int32, (SEQS, SEQS), 1)
    core_t, j_t, p_t, b_t = t >> 6, (t >> 4) & 3, (t >> 3) & 1, t & 7
    a_t = (even_a + core_t + (2 * core_t - 1) * j_t) & 7
    seq_t = jnp.where(half == 0, b_t * 16 + a_t * 2, a_t * 16 + b_t * 2) + p_t
    order = (lax.broadcasted_iota(jnp.int32, (SEQS, SEQS), 0) == seq_t).astype(BF16)
    live_bits = jnp.broadcast_to((smask[...] > 0).astype(BF16), (16, SEQS))
    seq_keys = dot_nn(live_bits, order)[:1] > 0.5
    bytes_of(arx, aa_r.at[0]).wait()
    bytes_of(rxc, cx_r.at[0]).wait()

    arrived = rxc[...].reshape(32, 2 * D)
    context = jnp.concatenate(
        [
            jnp.concatenate(
                [
                    arrived[8 * i : 8 * i + 8, 512 * h + HEAD * jp : 512 * h + HEAD * jp + HEAD]
                    for i in range(4)
                    for h in range(3)
                ],
                axis=1,
            )
            for jp in range(8)
        ],
        axis=0,
    ).astype(BF16)
    three_halves(0, wf_r).wait()
    rows = rounded(arx[...].reshape(64, D) + dot_nt(context, wfull[0]))
    col_normed = normalize(rows, 1)
    own_rows = pl.ds(pl.multiple_of(64 * c, 64), 64)
    three_halves(1, wf_r).wait()
    kf[own_rows, :] = dot_nt(col_normed, wfull[1]).astype(BF16)
    kcopy = remote(kf.at[own_rows, :], kf.at[own_rows, :], kv_s.at[0], kv_r.at[0], sibling)
    kcopy.start()
    three_halves(2, wf_r).wait()
    vf[own_rows, :] = dot_nt(col_normed, wfull[2]).astype(BF16)
    vcopy = remote(vf.at[own_rows, :], vf.at[own_rows, :], kv_s.at[1], kv_r.at[1], sibling)
    vcopy.start()
    forward(4)
    three_halves(3, wf_r).wait()
    col_queries = rounded(dot_nt(col_normed, wfull[3]))
    kcopy.wait_recv()
    low = lax.broadcasted_iota(jnp.int32, (64, 128), 1) < HEAD
    col_context = []
    for p in range(6):
        cols = slice(128 * p, 128 * p + 128)
        pair = col_queries[:, cols]
        stacked = jnp.concatenate([jnp.where(low, pair, 0.0), jnp.where(low, 0.0, pair)], axis=0).astype(BF16)
        col_probs = softmax(dot_nt(stacked, kf[:, cols]) * COL_SCALE, seq_keys)
        if p == 0:
            vcopy.wait_recv()
        result = dot_nn(col_probs, vf[:, cols])
        col_context.append(jnp.where(low, result[:64], result[64:]))
    col_context = jnp.concatenate(col_context, axis=1).astype(BF16)
    three_halves(4, wf_r).wait()
    mrow[...] = rounded(rows + dot_nt(col_context, wfull[4])).reshape(64, 1, D)

    for db in (4, 3, 5, 2, 6, 1, 7, 0):
        b = (own_b + db) & 7
        for j in (3, 2, 1, 0):
            a = (even_a + c + (2 * c - 1) * j) & 7
            for dp in range(2):
                p = c ^ dp
                to_device(
                    home if db == j == dp == 0 else None,
                    mrow.at[(2 * j + p) * 8 + b], mrx.at[own_n], bb_s.at[0], bb_r.at[0],
                    (a * a_step + b * b_step + p, x),
                )

    for k in range(3):
        bytes_of(ag.at[0], xs_s.at[k]).wait()
    for i in range(5):
        three_halves(i, wg_s).wait()
        three_halves(i, wf_s).wait()
    bytes_of(vall.at[1:4], vg_s.at[0]).wait()
    for copies in (scatters, spreads):
        for copy in copies.values():
            copy.wait_send()
    for copy in swaps + [paired, kcopy, vcopy]:
        copy.wait_send()
    wait_rows_sent(srow, 64, home, aa_s.at[0])
    wait_rows_sent(msg, 32, jnp.logical_and(odd == c, half == c), cx_s.at[0])

    bytes_of(mrx, bb_r.at[0]).wait()
    placed = mrx[...].reshape(64, D)
    for i in range(4):
        xb[i] = placed[:, PART * i : PART * i + PART].astype(BF16)
    returns = {}
    for k in (2, 1, 3):
        other = (x + k) & 3
        returns[k] = remote(xb.at[other], xr.at[x], ox_s.at[k - 1], ox_r.at[k - 1], dev(z, y, c, other))
        returns[k].start()
    xr[x] = xb[x]
    place = lax.broadcasted_iota(jnp.int32, (128, 128), 0)
    spread = (lax.broadcasted_iota(jnp.int32, (128, 128), 1) == 2 * (place & 63) + (place >> 6)).astype(BF16)
    wait_rows_sent(mrow, 64, home, bb_s.at[0])
    for k in (1, 3, 2):
        returns[k].wait_recv()
    for i in range(2):
        both = jnp.concatenate([xr[2 * i], xr[2 * i + 1]], axis=0)
        out[0, :, 128 * i : 128 * i + 128] = dot_tn(both, spread).astype(BF16)
    for copy in returns.values():
        copy.wait_send()


def shards(
    alignment,
    row_query_key,
    row_value,
    row_output,
    col_query_key,
    col_value,
    col_output,
    sequence_mask,
    residue_mask,
):
    dma = pltpu.SemaphoreType.DMA
    in_hbm = pl.BlockSpec(memory_space=pltpu.HBM)
    in_vmem = pl.BlockSpec(memory_space=pltpu.VMEM)
    return pl.pallas_call(
        layer,
        out_shape=jax.ShapeDtypeStruct((1, PART, L), BF16),
        in_specs=[in_hbm] * 9,
        out_specs=in_vmem,
        scratch_shapes=[
            pltpu.VMEM((1, SEQS), jnp.int32),
            pltpu.VMEM((1, L), jnp.int32),
            pltpu.VMEM((4, PART, L), BF16),
            pltpu.VMEM((3, PART, D), BF16),
            pltpu.VMEM((5, D, D), BF16),
            pltpu.VMEM((2, PART, 128), BF16),
            pltpu.VMEM((PART, L), BF16),
            pltpu.VMEM((4, 2, PART, L), BF16),
            pltpu.VMEM((PART, 128), BF16),
            pltpu.VMEM((PART, L), BF16),
            pltpu.VMEM((384, L), F32),
            pltpu.VMEM((8, 48, L), F32),
            pltpu.VMEM((8, 48, L), BF16),
            pltpu.VMEM((7, 48, L), BF16),
            pltpu.VMEM((48, L), BF16),
            pltpu.VMEM((7, 48, L), BF16),
            pltpu.VMEM((2, 48, L), BF16),
            pltpu.VMEM((32, 1, 2 * D), F32),
            pltpu.VMEM((32, 1, 2 * D), F32),
            pltpu.VMEM((64, 1, D), F32),
            pltpu.VMEM((64, 1, D), F32),
            pltpu.VMEM((SEQS, D), BF16),
            pltpu.VMEM((SEQS, D), BF16),
            pltpu.VMEM((4, 64, PART), BF16),
            pltpu.VMEM((4, 64, PART), BF16),
            pltpu.VMEM((64, 1, D), F32),
            pltpu.VMEM((64, 1, D), F32),
            dma((11,)),
            pltpu.SemaphoreType.REGULAR((2,)),
            dma((3,)), dma((3,)),
            dma((5,)), dma((5, 3)),
            dma((5,)), dma((5,)),
            dma((3,)), dma((3,)),
            dma((7,)), dma((7,)),
            dma((7,)), dma((7,)),
            dma((1,)), dma((3, 2)),
            dma((1,)), dma((1,)),
            dma((1,)), dma((1,)),
            dma((1,)), dma((1,)),
            dma((2,)), dma((2,)),
            dma((3,)), dma((3,)),
            dma((1,)), dma((1,)),
        ],
        compiler_params=pltpu.CompilerParams(
            collective_id=0, has_side_effects=True, vmem_limit_bytes=60 << 20
        ),
        name="layer",
    )(
        alignment,
        row_query_key,
        row_value,
        row_output,
        col_query_key,
        col_value,
        col_output,
        sequence_mask.reshape(1, SEQS),
        residue_mask.reshape(1, L),
    )


def solution(mesh):
    placed = (
        P("seq", "head", None),
        P(None, "head", None),
        P("head", None),
        P("head", None),
        P(None, "head", None),
        P("head", None),
        P("head", None),
        P(),
        P(),
    )
    return jax.shard_map(
        shards, mesh=mesh, in_specs=placed, out_specs=P("seq", "head", None), check_vma=False
    )
```

```python
import math

import jax
import jax.numpy as jnp
from jax import lax
from jax.experimental import pallas as pl
from jax.experimental.pallas import tpu as pltpu
from jax.sharding import PartitionSpec as P

D = 768
HEADS = 12
L = 256
SEQS = 128
HEAD = D // HEADS
PART = D // 4
EPSILON = 1e-05
MASKED = -1e30
ROW_SCALE = HEAD**-0.5 / math.sqrt(SEQS)
COL_SCALE = HEAD**-0.5
MESH = pl.DeviceIdType.MESH
BF16 = jnp.bfloat16
F32 = jnp.float32
FAR = (4, 3, 5, 2, 6, 1, 7)
NEAR = FAR[::-1]
BOTH_FAR = sorted(((a, b) for a in range(8) for b in range(8)), key=lambda d: -min(d[0], 8 - d[0]) - min(d[1], 8 - d[1]))


def dot_nt(a, b):
    return lax.dot_general(a, b, (((1,), (1,)), ((), ())), preferred_element_type=F32)


def dot_nn(a, b):
    return lax.dot_general(a, b, (((1,), (0,)), ((), ())), preferred_element_type=F32)


def dot_tn(a, b):
    return lax.dot_general(a, b, (((0,), (0,)), ((), ())), preferred_element_type=F32)


def normalize(values, axis):
    centred = values - jnp.mean(values, axis=axis, keepdims=True)
    variance = jnp.mean(centred * centred, axis=axis, keepdims=True)
    return (centred * lax.rsqrt(variance + EPSILON)).astype(BF16)


def softmax(logits, live):
    logits = jnp.where(live, logits, MASKED)
    weights = jnp.exp(logits - jnp.max(logits, axis=-1, keepdims=True))
    return (weights / jnp.sum(weights, axis=-1, keepdims=True)).astype(BF16)


def rounded(values):
    return values.astype(BF16).astype(F32)


def layer(
    al, rqk, rv, ro, cqk, cv, co, smask_hbm, rmask_hbm, out,
    smask, rmask,
    ag, wrow, wfull, qh, kk, vall, qrx, krx, pown, pacc, pb, ra, sb, rb, pp,
    msg, rxc, srow, arx, kf, vf, xb, xr, mrow, mrx,
    lsem, met, xs_s, xs_r, wg_s, wg_r, wf_s, wf_r, co_s, co_r, ra_s, ra_r, rb_s, rb_r,
    vg_s, vg_r, pr_s, pr_r, cx_s, cx_r, aa_s, aa_r, kv_s, kv_r, ox_s, ox_r, bb_s, bb_r,
):
    s = lax.axis_index("seq")
    x = lax.axis_index("head")
    z, y, c = s >> 4, (s >> 1) & 7, s & 1
    first = c == 0
    ia = jnp.where(first, y, z)
    ib = jnp.where(first, z, y)
    odd = ia & 1
    sign = 2 * odd - 1
    half = x >> 1
    own_a = jnp.where(half == 0, y, z)
    own_b = jnp.where(half == 0, z, y)
    own_n = own_a * 8 + own_b
    even_a = own_a & 6
    home = (own_a & 1) == c
    a_step = jnp.where(half == 0, 2, 16)
    b_step = jnp.where(half == 0, 16, 2)

    def dev(z_, y_, c_, x_):
        return (z_ * 16 + y_ * 2 + c_, x_)

    def dev_a(g):
        return dev(jnp.where(first, z, g), jnp.where(first, g, y), c, x)

    def dev_b(g):
        return dev(jnp.where(first, g, z), jnp.where(first, y, g), c, x)

    def remote(src, dst, ss, rs, target):
        return pltpu.make_async_remote_copy(
            src_ref=src, dst_ref=dst, send_sem=ss, recv_sem=rs, device_id=target, device_id_type=MESH
        )

    def bytes_of(ref, sem):
        return pltpu.make_async_copy(ref, ref, sem)

    def to_device(here, src, dst, ss, rs, target):
        if here is None:
            remote(src, dst, ss, rs, target).start()
            return

        @pl.when(here)
        def _():
            pltpu.make_async_copy(src, dst, rs).start()

        @pl.when(jnp.logical_not(here))
        def _():
            remote(src, dst, ss, rs, target).start()

    def wait_rows_sent(ref, count, one_stays, sem):
        @pl.when(one_stays)
        def _():
            bytes_of(ref.at[: count - 1], sem).wait()

        @pl.when(jnp.logical_not(one_stays))
        def _():
            bytes_of(ref, sem).wait()

    sibling = dev(z, y, 1 - c, x)

    barrier = pltpu.get_barrier_semaphore()
    ring = [dev_a((ia + k) & 7) for k in FAR] + [dev_b((ib + k) & 7) for k in FAR]
    greeted = ring + [dev(z, y, c ^ j, (x + k) & 3) for k in range(4) for j in range(2) if j or k]
    loads = [pltpu.make_async_copy(al.at[0], ag.at[x], lsem.at[0])]
    loads[0].start()
    for target in greeted:
        pl.semaphore_signal(barrier, inc=1, device_id=target, device_id_type=MESH)
    mine = pl.ds(pl.multiple_of(PART * x, 64), PART)
    weights = (ro, cqk.at[1], cv, cqk.at[0], co)
    for i, ref in enumerate((rqk.at[0], rqk.at[1], rv)):
        loads.append(pltpu.make_async_copy(ref, wrow.at[i], lsem.at[1 + i]))
    for i, ref in enumerate(weights):
        loads.append(pltpu.make_async_copy(ref, wfull.at[i, mine, :], lsem.at[4 + i]))
    loads.append(pltpu.make_async_copy(smask_hbm, smask, lsem.at[9]))
    loads.append(pltpu.make_async_copy(rmask_hbm, rmask, lsem.at[10]))
    for copy in loads[1:]:
        copy.start()
    loads[0].wait()
    pl.semaphore_wait(barrier, len(greeted))

    for j in range(4):
        for k in (2, 1, 3):
            part = ag.at[x, 48 * j : 48 * j + 48, :]
            remote(part, part, xs_s.at[k - 1], xs_r.at[k - 1], dev(z, y, c, (x + k) & 3)).start()
    for target in ring:
        pl.semaphore_signal(met.at[0], inc=1, device_id=target, device_id_type=MESH)
    pl.semaphore_wait(met.at[0], len(ring))
    pl.semaphore_signal(met.at[1], inc=1, device_id=sibling, device_id_type=MESH)
    pl.semaphore_wait(met.at[1], 1)
    for copy in loads[1:]:
        copy.wait()
    for k in (1, 3, 2):
        bytes_of(ag.at[0], xs_r.at[k - 1]).wait()

    onward = 1 - 2 * c
    after, before = dev(z, y, c, (x + onward) & 3), dev(z, y, c, (x - onward) & 3)

    def pieces(i, owner, ss, rs, target):
        for j in range(3):
            part = wfull.at[i, pl.ds(pl.multiple_of(PART * owner + 96 * c + 32 * j, 32), 32), :]
            remote(part, part, ss, rs, target).start()

    def gather_weights(i):
        pieces(i, x, wg_s.at[i], wg_r.at[i, 0], after)
        pieces(i, x, wg_s.at[i], wg_r.at[i, 1], before)

    def relay(i):
        bytes_of(wfull.at[i, :96, :], wg_r.at[i, 0]).wait()
        pieces(i, (x - onward) & 3, wg_s.at[i], wg_r.at[i, 2], after)

    def three_halves(i, sem):
        return bytes_of(wfull.at[i, :288, :], sem.at[i])

    def forward(i):
        bytes_of(wfull.at[i, :96, :], wg_r.at[i, 1]).wait()
        bytes_of(wfull.at[i, :96, :], wg_r.at[i, 2]).wait()
        for k in (1, 2, 3):
            rows = pl.ds(pl.multiple_of(PART * ((x - k) & 3) + 96 * c, 32), 96)
            part = wfull.at[i, rows, :]
            remote(part, part, wf_s.at[i], wf_r.at[i], sibling).start()

    def send_values(p):
        for piece in range(4):
            for j in (3, 2, 1):
                rows = pl.ds(48 * piece, 48)
                g = (ia + sign * (-j if j == 2 else j)) & 7
                remote(
                    vall.at[0, p, rows, :], vall.at[j, p, rows, :], vg_s.at[0], vg_r.at[j - 1, p], dev_a(g)
                ).start()

    floats = ag[...].reshape(D, L).astype(F32)
    normed = normalize(floats, 0)
    live = jnp.sum(
        jnp.where(lax.broadcasted_iota(jnp.int32, (1, SEQS), 1) == s, smask[...], 0), axis=-1, keepdims=True
    ).astype(F32)
    swaps = [
        remote(kk, krx, co_s.at[0], co_r.at[0], sibling),
        remote(qh.at[1 - c], qrx, co_s.at[1], co_r.at[1], sibling),
        remote(vall.at[0, c], vall.at[0, c], co_s.at[2], co_r.at[2], sibling),
    ]
    keys = dot_nn(wrow[1], normed).astype(BF16)
    kk[...] = keys
    swaps[0].start()
    queries = (dot_nn(wrow[0], normed) * live).astype(BF16)
    qh[0] = queries[:, :128]
    qh[1] = queries[:, 128:]
    swaps[1].start()
    vall[0, c] = dot_nn(wrow[2], normed).astype(BF16)
    swaps[2].start()
    send_values(c)
    for i in (0, 1):
        gather_weights(i)

    own_q = qh[c]
    for h in range(3):
        r = slice(HEAD * h, HEAD * h + HEAD)
        pown[128 * h : 128 * h + 128, :] = dot_tn(own_q[r], keys[r])
    swaps[0].wait_recv()
    swaps[1].wait_recv()
    for h in range(3):
        r = slice(HEAD * h, HEAD * h + HEAD)
        total = pown[128 * h : 128 * h + 128, :] + dot_tn(qrx[r, :], krx[r, :])
        for g in range(8):
            piece = total[16 * g : 16 * g + 16]
            pacc[g, 16 * h : 16 * h + 16, :] = piece
            pb[g, 16 * h : 16 * h + 16, :] = piece.astype(BF16)

    scatters = {}
    for k in FAR:
        g = (ia + k) & 7
        scatters[k] = remote(pb.at[g], ra.at[k - 1], ra_s.at[k - 1], ra_r.at[k - 1], dev_a(g))
        scatters[k].start()

    swaps[2].wait_recv()
    send_values(1 - c)

    for i in (2, 3, 4):
        gather_weights(i)

    pick = (
        lax.broadcasted_iota(jnp.int32, (64, L), 1)
        == 2 * lax.broadcasted_iota(jnp.int32, (64, L), 0) + (128 * half + (x & 1))
    ).astype(BF16)
    srow[...] = jnp.concatenate([dot_nt(pick, ag[i]) for i in range(4)], axis=1).reshape(64, 1, D)

    for k in NEAR:
        scatters[k].wait_recv()
    summed = pacc[ia]
    for k in range(7):
        summed = summed + ra[k].astype(F32)
    sb[...] = summed.astype(BF16)
    spreads = {}
    for k in FAR:
        spreads[k] = remote(sb, rb.at[k - 1], rb_s.at[k - 1], rb_r.at[k - 1], dev_b((ib + k) & 7))
        spreads[k].start()

    for i in range(4):
        relay(i)
    for da, db in BOTH_FAR:
        a, b = (own_a + da) & 7, (own_b + db) & 7
        d = (own_a - (a & 6)) & 7
        low = jnp.logical_or(d == 0, d >= 5)
        core = jnp.where(low, 0, 1)
        j = jnp.where(low, (8 - d) & 7, d - 1)
        to_device(
            home if da == db == 0 else None,
            srow.at[a * 8 + b], arx.at[(2 * j + c) * 8 + own_b], aa_s.at[0], aa_r.at[0],
            (a * a_step + b * b_step + core, x),
        )
    for k in NEAR:
        spreads[k].wait_recv()
    for k in range(7):
        summed = summed + rb[k].astype(F32)
    pp[odd] = softmax(summed * ROW_SCALE, rmask[...] > 0)
    paired = remote(pp.at[odd], pp.at[odd], pr_s.at[0], pr_r.at[0], dev_a(ia ^ 1))
    paired.start()
    for j in (1, 2, 3):
        for p in range(2):
            bytes_of(vall.at[j, p], vg_r.at[j - 1, p]).wait()

    def context_to_owners(parity, g, own):
        parts = []
        for h in range(3):
            r = slice(HEAD * h, HEAD * h + HEAD)
            values = jnp.concatenate([vall[j, p, r, :] for j in range(4) for p in range(2)], axis=0)
            parts.append(rounded(dot_nt(pp[parity, 16 * h : 16 * h + 16, :], values)))
        msg[pl.ds(16 * parity, 16)] = jnp.concatenate(parts, axis=1).reshape(16, 1, 2 * D)

        for db in (4, 3, 5, 2, 6, 1, 7, 0):
            b = (ib + db) & 7
            z_, y_ = jnp.where(first, b, g), jnp.where(first, g, b)
            for q in range(2):
                stays = jnp.logical_and(2 * c + q == x, odd == c) if own and db == 0 else None
                to_device(
                    stays, msg.at[16 * parity + 2 * b + q], rxc.at[x * 8 + ib], cx_s.at[0], cx_r.at[0],
                    dev(z_, y_, odd, 2 * c + q),
                )

    relay(4)
    context_to_owners(odd, ia, True)
    paired.wait_recv()
    context_to_owners(1 - odd, ia ^ 1, False)

    for i in range(4):
        forward(i)
    t = lax.broadcasted_iota(jnp.int32, (SEQS, SEQS), 1)
    core_t, j_t, p_t, b_t = t >> 6, (t >> 4) & 3, (t >> 3) & 1, t & 7
    a_t = (even_a + core_t + (2 * core_t - 1) * j_t) & 7
    seq_t = jnp.where(half == 0, b_t * 16 + a_t * 2, a_t * 16 + b_t * 2) + p_t
    order = (lax.broadcasted_iota(jnp.int32, (SEQS, SEQS), 0) == seq_t).astype(BF16)
    live_bits = jnp.broadcast_to((smask[...] > 0).astype(BF16), (16, SEQS))
    seq_keys = dot_nn(live_bits, order)[:1] > 0.5
    bytes_of(arx, aa_r.at[0]).wait()
    bytes_of(rxc, cx_r.at[0]).wait()

    arrived = rxc[...].reshape(32, 2 * D)
    context = jnp.concatenate(
        [
            jnp.concatenate(
                [
                    arrived[8 * i : 8 * i + 8, 512 * h + HEAD * jp : 512 * h + HEAD * jp + HEAD]
                    for i in range(4)
                    for h in range(3)
                ],
                axis=1,
            )
            for jp in range(8)
        ],
        axis=0,
    ).astype(BF16)
    three_halves(0, wf_r).wait()
    rows = rounded(arx[...].reshape(64, D) + dot_nt(context, wfull[0]))
    col_normed = normalize(rows, 1)
    own_rows = pl.ds(pl.multiple_of(64 * c, 64), 64)
    three_halves(1, wf_r).wait()
    kf[own_rows, :] = dot_nt(col_normed, wfull[1]).astype(BF16)
    kcopy = remote(kf.at[own_rows, :], kf.at[own_rows, :], kv_s.at[0], kv_r.at[0], sibling)
    kcopy.start()
    three_halves(2, wf_r).wait()
    vf[own_rows, :] = dot_nt(col_normed, wfull[2]).astype(BF16)
    vcopy = remote(vf.at[own_rows, :], vf.at[own_rows, :], kv_s.at[1], kv_r.at[1], sibling)
    vcopy.start()
    forward(4)
    three_halves(3, wf_r).wait()
    col_queries = rounded(dot_nt(col_normed, wfull[3]))
    kcopy.wait_recv()
    low = lax.broadcasted_iota(jnp.int32, (64, 128), 1) < HEAD
    col_probs = []
    for p in range(6):
        cols = slice(128 * p, 128 * p + 128)
        pair = col_queries[:, cols]
        stacked = jnp.concatenate([jnp.where(low, pair, 0.0), jnp.where(low, 0.0, pair)], axis=0).astype(BF16)
        col_probs.append(softmax(dot_nt(stacked, kf[:, cols]) * COL_SCALE, seq_keys))
    vcopy.wait_recv()
    col_context = []
    for p in range(6):
        result = dot_nn(col_probs[p], vf[:, 128 * p : 128 * p + 128])
        col_context.append(jnp.where(low, result[:64], result[64:]))
    col_context = jnp.concatenate(col_context, axis=1).astype(BF16)
    three_halves(4, wf_r).wait()
    mrow[...] = rounded(rows + dot_nt(col_context, wfull[4])).reshape(64, 1, D)

    for db in (4, 3, 5, 2, 6, 1, 7, 0):
        b = (own_b + db) & 7
        for j in (3, 2, 1, 0):
            a = (even_a + c + (2 * c - 1) * j) & 7
            for dp in range(2):
                p = c ^ dp
                to_device(
                    home if db == j == dp == 0 else None,
                    mrow.at[(2 * j + p) * 8 + b], mrx.at[own_n], bb_s.at[0], bb_r.at[0],
                    (a * a_step + b * b_step + p, x),
                )

    for k in range(3):
        bytes_of(ag.at[0], xs_s.at[k]).wait()
    for i in range(5):
        three_halves(i, wg_s).wait()
        three_halves(i, wf_s).wait()
    bytes_of(vall.at[1:4], vg_s.at[0]).wait()
    for copies in (scatters, spreads):
        for copy in copies.values():
            copy.wait_send()
    for copy in swaps + [paired, kcopy, vcopy]:
        copy.wait_send()
    wait_rows_sent(srow, 64, home, aa_s.at[0])
    wait_rows_sent(msg, 32, jnp.logical_and(odd == c, half == c), cx_s.at[0])

    bytes_of(mrx, bb_r.at[0]).wait()
    placed = mrx[...].reshape(64, D)
    for i in range(4):
        xb[i] = placed[:, PART * i : PART * i + PART].astype(BF16)
    returns = {}
    for k in (2, 1, 3):
        other = (x + k) & 3
        returns[k] = remote(xb.at[other], xr.at[x], ox_s.at[k - 1], ox_r.at[k - 1], dev(z, y, c, other))
        returns[k].start()
    xr[x] = xb[x]
    place = lax.broadcasted_iota(jnp.int32, (128, 128), 0)
    spread = (lax.broadcasted_iota(jnp.int32, (128, 128), 1) == 2 * (place & 63) + (place >> 6)).astype(BF16)
    wait_rows_sent(mrow, 64, home, bb_s.at[0])
    for k in (1, 3, 2):
        returns[k].wait_recv()
    for i in range(2):
        both = jnp.concatenate([xr[2 * i], xr[2 * i + 1]], axis=0)
        out[0, :, 128 * i : 128 * i + 128] = dot_tn(both, spread).astype(BF16)
    for copy in returns.values():
        copy.wait_send()


def shards(
    alignment,
    row_query_key,
    row_value,
    row_output,
    col_query_key,
    col_value,
    col_output,
    sequence_mask,
    residue_mask,
):
    dma = pltpu.SemaphoreType.DMA
    in_hbm = pl.BlockSpec(memory_space=pltpu.HBM)
    in_vmem = pl.BlockSpec(memory_space=pltpu.VMEM)
    return pl.pallas_call(
        layer,
        out_shape=jax.ShapeDtypeStruct((1, PART, L), BF16),
        in_specs=[in_hbm] * 9,
        out_specs=in_vmem,
        scratch_shapes=[
            pltpu.VMEM((1, SEQS), jnp.int32),
            pltpu.VMEM((1, L), jnp.int32),
            pltpu.VMEM((4, PART, L), BF16),
            pltpu.VMEM((3, PART, D), BF16),
            pltpu.VMEM((5, D, D), BF16),
            pltpu.VMEM((2, PART, 128), BF16),
            pltpu.VMEM((PART, L), BF16),
            pltpu.VMEM((4, 2, PART, L), BF16),
            pltpu.VMEM((PART, 128), BF16),
            pltpu.VMEM((PART, L), BF16),
            pltpu.VMEM((384, L), F32),
            pltpu.VMEM((8, 48, L), F32),
            pltpu.VMEM((8, 48, L), BF16),
            pltpu.VMEM((7, 48, L), BF16),
            pltpu.VMEM((48, L), BF16),
            pltpu.VMEM((7, 48, L), BF16),
            pltpu.VMEM((2, 48, L), BF16),
            pltpu.VMEM((32, 1, 2 * D), F32),
            pltpu.VMEM((32, 1, 2 * D), F32),
            pltpu.VMEM((64, 1, D), F32),
            pltpu.VMEM((64, 1, D), F32),
            pltpu.VMEM((SEQS, D), BF16),
            pltpu.VMEM((SEQS, D), BF16),
            pltpu.VMEM((4, 64, PART), BF16),
            pltpu.VMEM((4, 64, PART), BF16),
            pltpu.VMEM((64, 1, D), F32),
            pltpu.VMEM((64, 1, D), F32),
            dma((11,)),
            pltpu.SemaphoreType.REGULAR((2,)),
            dma((3,)), dma((3,)),
            dma((5,)), dma((5, 3)),
            dma((5,)), dma((5,)),
            dma((3,)), dma((3,)),
            dma((7,)), dma((7,)),
            dma((7,)), dma((7,)),
            dma((1,)), dma((3, 2)),
            dma((1,)), dma((1,)),
            dma((1,)), dma((1,)),
            dma((1,)), dma((1,)),
            dma((2,)), dma((2,)),
            dma((3,)), dma((3,)),
            dma((1,)), dma((1,)),
        ],
        compiler_params=pltpu.CompilerParams(
            collective_id=0, has_side_effects=True, vmem_limit_bytes=60 << 20
        ),
        name="layer",
    )(
        alignment,
        row_query_key,
        row_value,
        row_output,
        col_query_key,
        col_value,
        col_output,
        sequence_mask.reshape(1, SEQS),
        residue_mask.reshape(1, L),
    )


def solution(mesh):
    placed = (
        P("seq", "head", None),
        P(None, "head", None),
        P("head", None),
        P("head", None),
        P(None, "head", None),
        P("head", None),
        P("head", None),
        P(),
        P(),
    )
    return jax.shard_map(
        shards, mesh=mesh, in_specs=placed, out_specs=P("seq", "head", None), check_vma=False
    )
```

```python
import math

import jax
import jax.numpy as jnp
from jax import lax
from jax.experimental import pallas as pl
from jax.experimental.pallas import tpu as pltpu
from jax.sharding import PartitionSpec as P

D = 768
HEADS = 12
L = 256
SEQS = 128
HEAD = D // HEADS
PART = D // 4
EPSILON = 1e-05
MASKED = -1e30
ROW_SCALE = HEAD**-0.5 / math.sqrt(SEQS)
COL_SCALE = HEAD**-0.5
MESH = pl.DeviceIdType.MESH
BF16 = jnp.bfloat16
F32 = jnp.float32
FAR = (4, 3, 5, 2, 6, 1, 7)
NEAR = FAR[::-1]
BOTH_FAR = sorted(((a, b) for a in range(8) for b in range(8)), key=lambda d: -min(d[0], 8 - d[0]) - min(d[1], 8 - d[1]))


def dot_nt(a, b):
    return lax.dot_general(a, b, (((1,), (1,)), ((), ())), preferred_element_type=F32)


def dot_nn(a, b):
    return lax.dot_general(a, b, (((1,), (0,)), ((), ())), preferred_element_type=F32)


def dot_tn(a, b):
    return lax.dot_general(a, b, (((0,), (0,)), ((), ())), preferred_element_type=F32)


def normalize(values, axis):
    centred = values - jnp.mean(values, axis=axis, keepdims=True)
    variance = jnp.mean(centred * centred, axis=axis, keepdims=True)
    return (centred * lax.rsqrt(variance + EPSILON)).astype(BF16)


def softmax(logits, live):
    logits = jnp.where(live, logits, MASKED)
    weights = jnp.exp(logits - jnp.max(logits, axis=-1, keepdims=True))
    return (weights / jnp.sum(weights, axis=-1, keepdims=True)).astype(BF16)


def rounded(values):
    return values.astype(BF16).astype(F32)


def layer(
    al, rqk, rv, ro, cqk, cv, co, smask_hbm, rmask_hbm, out,
    smask, rmask,
    ag, wrow, wfull, qh, kk, vall, qrx, krx, pown, pacc, pb, ra, sb, rb, pp,
    msg, rxc, srow, arx, kf, vf, xb, xr, mrow, mrx,
    lsem, met, xs_s, xs_r, wg_s, wg_r, wf_s, wf_r, co_s, co_r, ra_s, ra_r, rb_s, rb_r,
    vg_s, vg_r, pr_s, pr_r, cx_s, cx_r, aa_s, aa_r, kv_s, kv_r, ox_s, ox_r, bb_s, bb_r,
):
    s = lax.axis_index("seq")
    x = lax.axis_index("head")
    z, y, c = s >> 4, (s >> 1) & 7, s & 1
    first = c == 0
    ia = jnp.where(first, y, z)
    ib = jnp.where(first, z, y)
    odd = ia & 1
    sign = 2 * odd - 1
    half = x >> 1
    own_a = jnp.where(half == 0, y, z)
    own_b = jnp.where(half == 0, z, y)
    own_n = own_a * 8 + own_b
    even_a = own_a & 6
    home = (own_a & 1) == c
    a_step = jnp.where(half == 0, 2, 16)
    b_step = jnp.where(half == 0, 16, 2)

    def dev(z_, y_, c_, x_):
        return (z_ * 16 + y_ * 2 + c_, x_)

    def dev_a(g):
        return dev(jnp.where(first, z, g), jnp.where(first, g, y), c, x)

    def dev_b(g):
        return dev(jnp.where(first, g, z), jnp.where(first, y, g), c, x)

    def remote(src, dst, ss, rs, target):
        return pltpu.make_async_remote_copy(
            src_ref=src, dst_ref=dst, send_sem=ss, recv_sem=rs, device_id=target, device_id_type=MESH
        )

    def bytes_of(ref, sem):
        return pltpu.make_async_copy(ref, ref, sem)

    def to_device(here, src, dst, ss, rs, target):
        if here is None:
            remote(src, dst, ss, rs, target).start()
            return

        @pl.when(here)
        def _():
            pltpu.make_async_copy(src, dst, rs).start()

        @pl.when(jnp.logical_not(here))
        def _():
            remote(src, dst, ss, rs, target).start()

    def wait_rows_sent(ref, count, one_stays, sem):
        @pl.when(one_stays)
        def _():
            bytes_of(ref.at[: count - 1], sem).wait()

        @pl.when(jnp.logical_not(one_stays))
        def _():
            bytes_of(ref, sem).wait()

    sibling = dev(z, y, 1 - c, x)

    barrier = pltpu.get_barrier_semaphore()
    ring = [dev_a((ia + k) & 7) for k in FAR] + [dev_b((ib + k) & 7) for k in FAR]
    greeted = ring + [dev(z, y, c ^ j, (x + k) & 3) for k in range(4) for j in range(2) if j or k]
    loads = [pltpu.make_async_copy(al.at[0], ag.at[x], lsem.at[0])]
    loads[0].start()
    for target in greeted:
        pl.semaphore_signal(barrier, inc=1, device_id=target, device_id_type=MESH)
    mine = pl.ds(pl.multiple_of(PART * x, 64), PART)
    weights = (ro, cqk.at[1], cv, cqk.at[0], co)
    for i, ref in enumerate((rqk.at[0], rqk.at[1], rv)):
        loads.append(pltpu.make_async_copy(ref, wrow.at[i], lsem.at[1 + i]))
    for i, ref in enumerate(weights):
        loads.append(pltpu.make_async_copy(ref, wfull.at[i, mine, :], lsem.at[4 + i]))
    loads.append(pltpu.make_async_copy(smask_hbm, smask, lsem.at[9]))
    loads.append(pltpu.make_async_copy(rmask_hbm, rmask, lsem.at[10]))
    for copy in loads[1:]:
        copy.start()
    loads[0].wait()
    pl.semaphore_wait(barrier, len(greeted))

    for j in range(4):
        for k in (2, 1, 3):
            part = ag.at[x, 48 * j : 48 * j + 48, :]
            remote(part, part, xs_s.at[k - 1], xs_r.at[k - 1], dev(z, y, c, (x + k) & 3)).start()
    for target in ring:
        pl.semaphore_signal(met.at[0], inc=1, device_id=target, device_id_type=MESH)
    pl.semaphore_wait(met.at[0], len(ring))
    pl.semaphore_signal(met.at[1], inc=1, device_id=sibling, device_id_type=MESH)
    pl.semaphore_wait(met.at[1], 1)
    for copy in loads[1:]:
        copy.wait()
    for k in (1, 3, 2):
        bytes_of(ag.at[0], xs_r.at[k - 1]).wait()

    onward = 1 - 2 * c
    after, before = dev(z, y, c, (x + onward) & 3), dev(z, y, c, (x - onward) & 3)

    def pieces(i, owner, ss, rs, target):
        for j in range(3):
            part = wfull.at[i, pl.ds(pl.multiple_of(PART * owner + 96 * c + 32 * j, 32), 32), :]
            remote(part, part, ss, rs, target).start()

    def gather_weights(i):
        pieces(i, x, wg_s.at[i], wg_r.at[i, 0], after)
        pieces(i, x, wg_s.at[i], wg_r.at[i, 1], before)

    def relay(i):
        bytes_of(wfull.at[i, :96, :], wg_r.at[i, 0]).wait()
        pieces(i, (x - onward) & 3, wg_s.at[i], wg_r.at[i, 2], after)

    def three_halves(i, sem):
        return bytes_of(wfull.at[i, :288, :], sem.at[i])

    def forward(i):
        bytes_of(wfull.at[i, :96, :], wg_r.at[i, 1]).wait()
        bytes_of(wfull.at[i, :96, :], wg_r.at[i, 2]).wait()
        for k in (1, 2, 3):
            rows = pl.ds(pl.multiple_of(PART * ((x - k) & 3) + 96 * c, 32), 96)
            part = wfull.at[i, rows, :]
            remote(part, part, wf_s.at[i], wf_r.at[i], sibling).start()

    def send_values(p):
        for piece in range(4):
            for j in (3, 2, 1):
                rows = pl.ds(48 * piece, 48)
                g = (ia + sign * (-j if j == 2 else j)) & 7
                remote(
                    vall.at[0, p, rows, :], vall.at[j, p, rows, :], vg_s.at[0], vg_r.at[j - 1, p], dev_a(g)
                ).start()

    floats = ag[...].reshape(D, L).astype(F32)
    normed = normalize(floats, 0)
    live = jnp.sum(
        jnp.where(lax.broadcasted_iota(jnp.int32, (1, SEQS), 1) == s, smask[...], 0), axis=-1, keepdims=True
    ).astype(F32)
    swaps = [
        remote(kk, krx, co_s.at[0], co_r.at[0], sibling),
        remote(qh.at[1 - c], qrx, co_s.at[1], co_r.at[1], sibling),
        remote(vall.at[0, c], vall.at[0, c], co_s.at[2], co_r.at[2], sibling),
    ]
    projected = dot_nn(wrow[:2].reshape(2 * PART, D), normed)
    keys = projected[PART:].astype(BF16)
    kk[...] = keys
    swaps[0].start()
    queries = (projected[:PART] * live).astype(BF16)
    qh[0] = queries[:, :128]
    qh[1] = queries[:, 128:]
    swaps[1].start()
    vall[0, c] = dot_nn(wrow[2], normed).astype(BF16)
    swaps[2].start()
    send_values(c)
    for i in (0, 1):
        gather_weights(i)

    own_q = qh[c]
    for h in range(3):
        r = slice(HEAD * h, HEAD * h + HEAD)
        pown[128 * h : 128 * h + 128, :] = dot_tn(own_q[r], keys[r])
    swaps[0].wait_recv()
    swaps[1].wait_recv()
    for h in range(3):
        r = slice(HEAD * h, HEAD * h + HEAD)
        total = pown[128 * h : 128 * h + 128, :] + dot_tn(qrx[r, :], krx[r, :])
        for g in range(8):
            piece = total[16 * g : 16 * g + 16]
            pacc[g, 16 * h : 16 * h + 16, :] = piece
            pb[g, 16 * h : 16 * h + 16, :] = piece.astype(BF16)

    scatters = {}
    for k in FAR:
        g = (ia + k) & 7
        scatters[k] = remote(pb.at[g], ra.at[k - 1], ra_s.at[k - 1], ra_r.at[k - 1], dev_a(g))
        scatters[k].start()

    swaps[2].wait_recv()
    send_values(1 - c)

    for i in (2, 3, 4):
        gather_weights(i)

    pick = (
        lax.broadcasted_iota(jnp.int32, (64, L), 1)
        == 2 * lax.broadcasted_iota(jnp.int32, (64, L), 0) + (128 * half + (x & 1))
    ).astype(BF16)
    srow[...] = jnp.concatenate([dot_nt(pick, ag[i]) for i in range(4)], axis=1).reshape(64, 1, D)

    for k in NEAR:
        scatters[k].wait_recv()
    summed = pacc[ia]
    for k in range(7):
        summed = summed + ra[k].astype(F32)
    sb[...] = summed.astype(BF16)
    spreads = {}
    for k in FAR:
        spreads[k] = remote(sb, rb.at[k - 1], rb_s.at[k - 1], rb_r.at[k - 1], dev_b((ib + k) & 7))
        spreads[k].start()

    for i in range(4):
        relay(i)
    for da, db in BOTH_FAR:
        a, b = (own_a + da) & 7, (own_b + db) & 7
        d = (own_a - (a & 6)) & 7
        low = jnp.logical_or(d == 0, d >= 5)
        core = jnp.where(low, 0, 1)
        j = jnp.where(low, (8 - d) & 7, d - 1)
        to_device(
            home if da == db == 0 else None,
            srow.at[a * 8 + b], arx.at[(2 * j + c) * 8 + own_b], aa_s.at[0], aa_r.at[0],
            (a * a_step + b * b_step + core, x),
        )
    for k in NEAR:
        spreads[k].wait_recv()
    for k in range(7):
        summed = summed + rb[k].astype(F32)
    pp[odd] = softmax(summed * ROW_SCALE, rmask[...] > 0)
    paired = remote(pp.at[odd], pp.at[odd], pr_s.at[0], pr_r.at[0], dev_a(ia ^ 1))
    paired.start()
    for j in (1, 2, 3):
        for p in range(2):
            bytes_of(vall.at[j, p], vg_r.at[j - 1, p]).wait()

    def context_to_owners(parity, g, own):
        parts = []
        for h in range(3):
            r = slice(HEAD * h, HEAD * h + HEAD)
            values = jnp.concatenate([vall[j, p, r, :] for j in range(4) for p in range(2)], axis=0)
            parts.append(rounded(dot_nt(pp[parity, 16 * h : 16 * h + 16, :], values)))
        msg[pl.ds(16 * parity, 16)] = jnp.concatenate(parts, axis=1).reshape(16, 1, 2 * D)

        for db in (4, 3, 5, 2, 6, 1, 7, 0):
            b = (ib + db) & 7
            z_, y_ = jnp.where(first, b, g), jnp.where(first, g, b)
            for q in range(2):
                stays = jnp.logical_and(2 * c + q == x, odd == c) if own and db == 0 else None
                to_device(
                    stays, msg.at[16 * parity + 2 * b + q], rxc.at[x * 8 + ib], cx_s.at[0], cx_r.at[0],
                    dev(z_, y_, odd, 2 * c + q),
                )

    relay(4)
    context_to_owners(odd, ia, True)
    paired.wait_recv()
    context_to_owners(1 - odd, ia ^ 1, False)

    for i in range(4):
        forward(i)
    t = lax.broadcasted_iota(jnp.int32, (SEQS, SEQS), 1)
    core_t, j_t, p_t, b_t = t >> 6, (t >> 4) & 3, (t >> 3) & 1, t & 7
    a_t = (even_a + core_t + (2 * core_t - 1) * j_t) & 7
    seq_t = jnp.where(half == 0, b_t * 16 + a_t * 2, a_t * 16 + b_t * 2) + p_t
    order = (lax.broadcasted_iota(jnp.int32, (SEQS, SEQS), 0) == seq_t).astype(BF16)
    live_bits = jnp.broadcast_to((smask[...] > 0).astype(BF16), (16, SEQS))
    seq_keys = dot_nn(live_bits, order)[:1] > 0.5
    bytes_of(arx, aa_r.at[0]).wait()
    bytes_of(rxc, cx_r.at[0]).wait()

    arrived = rxc[...].reshape(32, 2 * D)
    context = jnp.concatenate(
        [
            jnp.concatenate(
                [
                    arrived[8 * i : 8 * i + 8, 512 * h + HEAD * jp : 512 * h + HEAD * jp + HEAD]
                    for i in range(4)
                    for h in range(3)
                ],
                axis=1,
            )
            for jp in range(8)
        ],
        axis=0,
    ).astype(BF16)
    three_halves(0, wf_r).wait()
    rows = rounded(arx[...].reshape(64, D) + dot_nt(context, wfull[0]))
    col_normed = normalize(rows, 1)
    own_rows = pl.ds(pl.multiple_of(64 * c, 64), 64)
    three_halves(1, wf_r).wait()
    kf[own_rows, :] = dot_nt(col_normed, wfull[1]).astype(BF16)
    kcopy = remote(kf.at[own_rows, :], kf.at[own_rows, :], kv_s.at[0], kv_r.at[0], sibling)
    kcopy.start()
    three_halves(2, wf_r).wait()
    vf[own_rows, :] = dot_nt(col_normed, wfull[2]).astype(BF16)
    vcopy = remote(vf.at[own_rows, :], vf.at[own_rows, :], kv_s.at[1], kv_r.at[1], sibling)
    vcopy.start()
    forward(4)
    three_halves(3, wf_r).wait()
    col_queries = rounded(dot_nt(col_normed, wfull[3]))
    kcopy.wait_recv()
    low = lax.broadcasted_iota(jnp.int32, (64, 128), 1) < HEAD
    col_probs = []
    for p in range(6):
        cols = slice(128 * p, 128 * p + 128)
        pair = col_queries[:, cols]
        stacked = jnp.concatenate([jnp.where(low, pair, 0.0), jnp.where(low, 0.0, pair)], axis=0).astype(BF16)
        col_probs.append(softmax(dot_nt(stacked, kf[:, cols]) * COL_SCALE, seq_keys))
    vcopy.wait_recv()
    col_context = []
    for p in range(6):
        result = dot_nn(col_probs[p], vf[:, 128 * p : 128 * p + 128])
        col_context.append(jnp.where(low, result[:64], result[64:]))
    col_context = jnp.concatenate(col_context, axis=1).astype(BF16)
    three_halves(4, wf_r).wait()
    mrow[...] = rounded(rows + dot_nt(col_context, wfull[4])).reshape(64, 1, D)

    for db in (4, 3, 5, 2, 6, 1, 7, 0):
        b = (own_b + db) & 7
        for j in (3, 2, 1, 0):
            a = (even_a + c + (2 * c - 1) * j) & 7
            for dp in range(2):
                p = c ^ dp
                to_device(
                    home if db == j == dp == 0 else None,
                    mrow.at[(2 * j + p) * 8 + b], mrx.at[own_n], bb_s.at[0], bb_r.at[0],
                    (a * a_step + b * b_step + p, x),
                )

    for k in range(3):
        bytes_of(ag.at[0], xs_s.at[k]).wait()
    for i in range(5):
        three_halves(i, wg_s).wait()
        three_halves(i, wf_s).wait()
    bytes_of(vall.at[1:4], vg_s.at[0]).wait()
    for copies in (scatters, spreads):
        for copy in copies.values():
            copy.wait_send()
    for copy in swaps + [paired, kcopy, vcopy]:
        copy.wait_send()
    wait_rows_sent(srow, 64, home, aa_s.at[0])
    wait_rows_sent(msg, 32, jnp.logical_and(odd == c, half == c), cx_s.at[0])

    bytes_of(mrx, bb_r.at[0]).wait()
    placed = mrx[...].reshape(64, D)
    for i in range(4):
        xb[i] = placed[:, PART * i : PART * i + PART].astype(BF16)
    returns = {}
    for k in (2, 1, 3):
        other = (x + k) & 3
        returns[k] = remote(xb.at[other], xr.at[x], ox_s.at[k - 1], ox_r.at[k - 1], dev(z, y, c, other))
        returns[k].start()
    xr[x] = xb[x]
    place = lax.broadcasted_iota(jnp.int32, (128, 128), 0)
    spread = (lax.broadcasted_iota(jnp.int32, (128, 128), 1) == 2 * (place & 63) + (place >> 6)).astype(BF16)
    wait_rows_sent(mrow, 64, home, bb_s.at[0])
    for k in (1, 3, 2):
        returns[k].wait_recv()
    for i in range(2):
        both = jnp.concatenate([xr[2 * i], xr[2 * i + 1]], axis=0)
        out[0, :, 128 * i : 128 * i + 128] = dot_tn(both, spread).astype(BF16)
    for copy in returns.values():
        copy.wait_send()


def shards(
    alignment,
    row_query_key,
    row_value,
    row_output,
    col_query_key,
    col_value,
    col_output,
    sequence_mask,
    residue_mask,
):
    dma = pltpu.SemaphoreType.DMA
    in_hbm = pl.BlockSpec(memory_space=pltpu.HBM)
    in_vmem = pl.BlockSpec(memory_space=pltpu.VMEM)
    return pl.pallas_call(
        layer,
        out_shape=jax.ShapeDtypeStruct((1, PART, L), BF16),
        in_specs=[in_hbm] * 9,
        out_specs=in_vmem,
        scratch_shapes=[
            pltpu.VMEM((1, SEQS), jnp.int32),
            pltpu.VMEM((1, L), jnp.int32),
            pltpu.VMEM((4, PART, L), BF16),
            pltpu.VMEM((3, PART, D), BF16),
            pltpu.VMEM((5, D, D), BF16),
            pltpu.VMEM((2, PART, 128), BF16),
            pltpu.VMEM((PART, L), BF16),
            pltpu.VMEM((4, 2, PART, L), BF16),
            pltpu.VMEM((PART, 128), BF16),
            pltpu.VMEM((PART, L), BF16),
            pltpu.VMEM((384, L), F32),
            pltpu.VMEM((8, 48, L), F32),
            pltpu.VMEM((8, 48, L), BF16),
            pltpu.VMEM((7, 48, L), BF16),
            pltpu.VMEM((48, L), BF16),
            pltpu.VMEM((7, 48, L), BF16),
            pltpu.VMEM((2, 48, L), BF16),
            pltpu.VMEM((32, 1, 2 * D), F32),
            pltpu.VMEM((32, 1, 2 * D), F32),
            pltpu.VMEM((64, 1, D), F32),
            pltpu.VMEM((64, 1, D), F32),
            pltpu.VMEM((SEQS, D), BF16),
            pltpu.VMEM((SEQS, D), BF16),
            pltpu.VMEM((4, 64, PART), BF16),
            pltpu.VMEM((4, 64, PART), BF16),
            pltpu.VMEM((64, 1, D), F32),
            pltpu.VMEM((64, 1, D), F32),
            dma((11,)),
            pltpu.SemaphoreType.REGULAR((2,)),
            dma((3,)), dma((3,)),
            dma((5,)), dma((5, 3)),
            dma((5,)), dma((5,)),
            dma((3,)), dma((3,)),
            dma((7,)), dma((7,)),
            dma((7,)), dma((7,)),
            dma((1,)), dma((3, 2)),
            dma((1,)), dma((1,)),
            dma((1,)), dma((1,)),
            dma((1,)), dma((1,)),
            dma((2,)), dma((2,)),
            dma((3,)), dma((3,)),
            dma((1,)), dma((1,)),
        ],
        compiler_params=pltpu.CompilerParams(
            collective_id=0, has_side_effects=True, vmem_limit_bytes=60 << 20
        ),
        name="layer",
    )(
        alignment,
        row_query_key,
        row_value,
        row_output,
        col_query_key,
        col_value,
        col_output,
        sequence_mask.reshape(1, SEQS),
        residue_mask.reshape(1, L),
    )


def solution(mesh):
    placed = (
        P("seq", "head", None),
        P(None, "head", None),
        P("head", None),
        P("head", None),
        P(None, "head", None),
        P("head", None),
        P("head", None),
        P(),
        P(),
    )
    return jax.shard_map(
        shards, mesh=mesh, in_specs=placed, out_specs=P("seq", "head", None), check_vma=False
    )
```
